512 devices in a mesh: pulse: 128 (over y, z, x_hi), rng: 4 (over x_lo, core).
Axes of the slice: x: 4 (x_hi: 2, x_lo: 2; x = x_hi * 2 + x_lo), y: 4, z: 16, core: 2. Of those that a mesh axis runs over, the one named last changes fastest.
Arguments:
- echoes: bfloat16 [2, 16384, 8192], P(None, 'pulse', 'rng'), may hold values from -6 to 6
- range_ref: bfloat16 [2, 1024], replicated, may hold values from -0.125 to 0.125
- band_weights: bfloat16 [64, 8192], P(None, 'rng'), may hold values from -0.75 to 0.75
- band_offsets: int32 [8192], P('rng'), may hold values from 0 to 32, as said below
- azimuth_ref: bfloat16 [2, 512], replicated, may hold values from -0.1875 to 0.1875
Outputs:
- image: float32 [2, 4, 2048, 16384], P(None, 'rng', 'pulse')
The draws below stay inside these ranges and needn't reach their ends.
Inputs may be any that keep to these rules, and one draw needn't show every extreme that they name: `band_offsets`: every value from 0 to one half of 64 may occur; both ends occur in every draw.
All inputs are finite; a program needn't handle non-finite values.
Results may differ from the reference program's by a relative error of at most 0.0041.
Values may be sent and summed in bfloat16 or wider, within the bound.
A program may use at most 64 MiB of HBM per device.

```python
import math
from functools import partial
import jax
import jax.numpy as jnp
from jax import lax

R = 8192
RT = 1024
AT = 512
BAND = 64
BLK = 128
PULSES = 16384
N_RNG = 4


def draw_band_offsets(key, part):
    key_values, key_high, key_low = jax.random.split(jax.random.fold_in(key, 17), 3)
    values = jax.random.randint(key_values, (R,), 0, BAND // 2 + 1)
    high_spot = jax.random.randint(key_high, (), 0, R)
    low_spot = jax.random.randint(key_low, (), 0, R)
    positions = jnp.arange(R)
    values = jnp.where(positions == high_spot, BAND // 2, values)
    values = jnp.where((positions == low_spot) & (positions != high_spot), 0, values)
    return values.astype(jnp.int32)


def block_scale(key, dims, cuts, low, high):
    def one(dim, parts):
        steps = jax.random.uniform(jax.random.fold_in(jax.random.fold_in(key, 6), dim), (parts,), jnp.float32, low / len(cuts), high / len(cuts))
        return jnp.repeat(jnp.exp(steps), dims[dim] // parts).reshape((-1,) + (1,) * (len(dims) - dim - 1))

    factor_of = one(*cuts[0])
    for cut in cuts[1:]:
        factor_of = factor_of * one(*cut)
    return factor_of


def centred(key, dims, spread, limit, pieces=(), held_as=jnp.bfloat16):
    entries = spread * jax.random.normal(key, dims, jnp.float32)
    if pieces:
        entries = entries * block_scale(key, dims, pieces, -0.22, 0.18)
    return jnp.clip(entries, -limit, limit).astype(held_as)


def setup_inputs(seed: int = 0) -> dict:
    arg_keys = jax.random.split(jax.random.key(seed), 6)
    return {
        "echoes": centred(arg_keys[0], (2, PULSES, R), 1.0, 6.0, ((1, 128), (2, 4))),
        "range_ref": centred(arg_keys[1], (2, RT), (2 * RT) ** -0.5, 0.125),
        "band_weights": centred(arg_keys[2], (BAND, R), BAND ** -0.5, 0.75, ((1, 4),)),
        "band_offsets": draw_band_offsets(jax.random.fold_in(arg_keys[5], 71), 0),
        "azimuth_ref": centred(arg_keys[4], (2, AT), (2 * AT) ** -0.5, 0.1875),
    }


def toeplitz_real(filter_taps, block_count):
    tap_total = filter_taps.shape[1]
    in_index = jnp.arange(BLK, dtype=jnp.int32)[:, None]
    out_index = jnp.arange(BLK, dtype=jnp.int32)[None, :]
    tap_index = (jnp.arange(block_count, dtype=jnp.int32) * BLK)[:, None, None] + in_index - out_index
    usable = (tap_index >= 0) & (tap_index < tap_total)
    clipped = jnp.clip(tap_index, 0, tap_total - 1)
    zero_tap = jnp.zeros((), filter_taps.dtype)
    real_part = jnp.where(usable, filter_taps[0][clipped], zero_tap)
    imag_part = jnp.where(usable, filter_taps[1][clipped], zero_tap)
    upper = jnp.stack([real_part, -imag_part], axis=2)
    lower = jnp.stack([imag_part, real_part], axis=2)
    return jnp.stack([upper, lower], axis=1)


def correlate_ref(blocks, kernel, out_blocks):
    running = None
    for tap_block in range(kernel.shape[0]):
        window = blocks[:, :, tap_block:tap_block + out_blocks].astype(jnp.float32)
        partial_sum = jnp.einsum("zrbi,ziwc->wrbc", window, kernel[tap_block].astype(jnp.float32), precision=lax.Precision.HIGHEST)
        running = partial_sum if running is None else running + partial_sum
    return running


def grouped_correlate(blocks, kernel, out_blocks):
    row_total = blocks.shape[1]
    group_size = math.gcd(row_total, 256)
    stacked = blocks.reshape(2, row_total // group_size, group_size, blocks.shape[2], BLK).transpose(1, 0, 2, 3, 4)
    outputs = lax.map(partial(correlate_ref, kernel=kernel, out_blocks=out_blocks), stacked)
    return outputs.transpose(1, 0, 2, 3, 4).reshape(2, row_total, out_blocks, BLK)


def band_matrices(weights_t, offsets, block_total):
    table = weights_t.reshape(BAND, block_total, BLK).transpose(1, 0, 2)
    shifts = offsets.reshape(block_total, 1, BLK).astype(jnp.int32)
    in_index = jnp.arange(2 * BLK, dtype=jnp.int32)[None, :, None]
    out_index = jnp.arange(BLK, dtype=jnp.int32)[None, None, :]
    tap_index = in_index - out_index - shifts - BAND // 2
    usable = (tap_index >= 0) & (tap_index < BAND)
    picked = jnp.take_along_axis(table, jnp.clip(tap_index, 0, BAND - 1), axis=1)
    return jnp.where(usable, picked, jnp.zeros((), table.dtype))


def migrate_padded(padded, weights_t, offsets):
    block_total = offsets.shape[0] // BLK
    matrices = band_matrices(weights_t, offsets, block_total).astype(jnp.float32)
    pulse_total = padded.shape[1]
    tiles = padded.reshape(2, pulse_total, block_total + 1, BLK).astype(jnp.float32)
    lower = jnp.einsum("zrbi,bic->zbcr", tiles[:, :, :-1], matrices[:, :BLK], precision=lax.Precision.HIGHEST)
    upper = jnp.einsum("zrbi,bic->zbcr", tiles[:, :, 1:], matrices[:, BLK:], precision=lax.Precision.HIGHEST)
    return (lower + upper).reshape(2, block_total * BLK, pulse_total).astype(jnp.bfloat16)


def azimuth_focus(migrated, kernel):
    bin_total = migrated.shape[1]
    pulse_total = migrated.shape[2]
    padded = jnp.pad(migrated, ((0, 0), (0, 0), (AT // 2, AT // 2)))
    blocks = padded.reshape(2, bin_total, (pulse_total + AT) // BLK, BLK)
    return grouped_correlate(blocks, kernel, pulse_total // BLK).reshape(2, bin_total, pulse_total)


def reference(echoes, range_ref, band_weights, band_offsets, azimuth_ref):
    pulse_total = echoes.shape[1]
    range_kernel = toeplitz_real(range_ref, RT // BLK + 1)
    extended = jnp.pad(echoes, ((0, 0), (0, 0), (0, RT)))
    blocks = extended.reshape(2, pulse_total, (R + RT) // BLK, BLK)
    compressed = grouped_correlate(blocks, range_kernel, R // BLK).reshape(2, pulse_total, R).astype(jnp.bfloat16)
    padded = jnp.pad(compressed, ((0, 0), (0, 0), (BAND, BAND)))
    migrated = migrate_padded(padded, band_weights, band_offsets)
    focused = azimuth_focus(migrated, toeplitz_real(azimuth_ref, AT // BLK + 1))
    return focused.reshape(2, N_RNG, R // N_RNG, pulse_total)
```

```python
import jax
import jax.numpy as jnp
from jax import lax
from jax.experimental import pallas as pl
from jax.experimental.pallas import tpu as pltpu
from jax.sharding import PartitionSpec as P

MESH = pl.DeviceIdType.MESH
BLK = 128
PAIR = 2 * BLK
VMEM_BYTES = 40 * 1024 * 1024


def place_toeplitz(taps_ref, rows_ref, turned_ref, matrix_ref):
    chunks = taps_ref.shape[1] // BLK
    rows_ref[...] = jnp.zeros_like(rows_ref)
    for k in range(chunks):
        chunk = taps_ref[:, k * BLK : (k + 1) * BLK].astype(jnp.float32)
        rows_ref[2 * k : 2 * k + 2, BLK:PAIR] = chunk
        rows_ref[2 * k + 2 : 2 * k + 4, 0:BLK] = chunk
    source = lax.broadcasted_iota(jnp.int32, (PAIR, PAIR), 0)
    lane = lax.broadcasted_iota(jnp.int32, (PAIR, PAIR), 1)
    wanted = jnp.where(lane < BLK, BLK - lane, 3 * BLK - lane)
    turn = jnp.where(source == wanted, 1.0, 0.0).astype(jnp.bfloat16)
    turned_ref[...] = jnp.dot(
        rows_ref[...].astype(jnp.bfloat16), turn, preferred_element_type=jnp.float32
    )
    for k in range(chunks + 1):
        tiles = []
        for part in range(2):
            row = turned_ref[2 * k + part : 2 * k + part + 1, :]
            spread = jnp.broadcast_to(row, (BLK, PAIR))
            tiles.append(pltpu.roll(spread, 0, 1, stride=1, stride_axis=0)[:, :BLK])
        real, imag = tiles
        top = k * PAIR
        matrix_ref[top : top + BLK, 0:BLK] = real.astype(jnp.bfloat16)
        matrix_ref[top : top + BLK, BLK:PAIR] = (-imag).astype(jnp.bfloat16)
        matrix_ref[top + BLK : top + PAIR, 0:BLK] = imag.astype(jnp.bfloat16)
        matrix_ref[top + BLK : top + PAIR, BLK:PAIR] = real.astype(jnp.bfloat16)


def compress_kernel(
    pulse_peers,
    quarters,
    echoes,
    range_ref,
    weights,
    offsets,
    azimuth_ref,
    gathered,
    azimuth_matrix,
    own,
    right_halo,
    left_halo,
    joined,
    range_rows,
    range_turned,
    range_matrix,
    azimuth_rows,
    azimuth_turned,
    azimuth_held,
    compressed,
    outgoing,
    own_sem,
    halo_send_sem,
    halo_recv_sem,
    send_sem,
    recv_sem,
    local_sem,
    matrix_sem,
):
    me = lax.axis_index("pulse")
    quarter = lax.axis_index("rng")
    quarter_len = own.shape[2]
    blocks = quarter_len // BLK
    taps_blocks = range_ref.shape[1] // BLK
    depth = range_matrix.shape[0]
    has_right = quarter < quarters - 1
    has_left = quarter > 0

    barrier = pltpu.get_barrier_semaphore()

    @pl.when(has_right)
    def _():
        pl.semaphore_signal(barrier, inc=1, device_id=(me, quarter + 1), device_id_type=MESH)

    @pl.when(has_left)
    def _():
        pl.semaphore_signal(barrier, inc=1, device_id=(me, quarter - 1), device_id_type=MESH)

    def greet(step, carry):
        peer = lax.rem(me + step, pulse_peers)
        pl.semaphore_signal(barrier, inc=1, device_id=(peer, quarter), device_id_type=MESH)
        return carry

    lax.fori_loop(1, pulse_peers, greet, 0)

    load = pltpu.make_async_copy(echoes, own, own_sem)
    load.start()
    place_toeplitz(range_ref, range_rows, range_turned, range_matrix)
    load.wait()

    def join(source, first, count):
        for m in range(count):
            for part in range(2):
                at = (first + m) * PAIR + part * BLK
                joined[:, at : at + BLK] = source[part, :, m * BLK : (m + 1) * BLK]

    join(own, 1, blocks)

    neighbours = jnp.where(has_right, 1, 0) + jnp.where(has_left, 1, 0)
    pl.semaphore_wait(barrier, pulse_peers - 1 + neighbours)

    reach = right_halo.shape[2]
    to_left = pltpu.make_async_remote_copy(
        src_ref=echoes.at[:, :, pl.ds(0, reach)],
        dst_ref=right_halo,
        send_sem=halo_send_sem.at[0],
        recv_sem=halo_recv_sem.at[0],
        device_id=(me, quarter - 1),
        device_id_type=MESH,
    )
    to_right = pltpu.make_async_remote_copy(
        src_ref=echoes.at[:, :, pl.ds(quarter_len - BLK, BLK)],
        dst_ref=left_halo,
        send_sem=halo_send_sem.at[1],
        recv_sem=halo_recv_sem.at[1],
        device_id=(me, quarter + 1),
        device_id_type=MESH,
    )

    @pl.when(has_left)
    def _():
        to_left.start()

    @pl.when(has_right)
    def _():
        to_right.start()

    def compress(j):
        window = joined[:, pl.ds(pl.multiple_of((j + 1) * PAIR, PAIR), depth)]
        block = jnp.dot(window, range_matrix[...], preferred_element_type=jnp.float32)
        top = pl.multiple_of((j + 1) * BLK, BLK)
        compressed[pl.ds(top, BLK), 0:BLK] = block[:, 0:BLK].T.astype(jnp.bfloat16)
        compressed[pl.ds(top, BLK), BLK:PAIR] = block[:, BLK:PAIR].T.astype(jnp.bfloat16)

    def migrate(b):
        taps = weights.shape[0]
        table = weights[:, pl.ds(pl.multiple_of(b * BLK, BLK), BLK)].astype(jnp.float32)
        shift_row = offsets[pl.ds(b, 1), :].astype(jnp.float32)
        stacked = jnp.concatenate(
            [table, jnp.broadcast_to(shift_row, (BLK - taps, BLK))], axis=0
        ).T
        lane = lax.broadcasted_iota(jnp.int32, (BLK, BLK), 1)
        placed = jnp.where(lane < taps, stacked, 0.0)
        shifts = jnp.broadcast_to(stacked[:, taps : taps + 1], (BLK, BLK)).astype(jnp.int32)
        step = 1
        while step <= taps // 2:
            moved = pltpu.roll(placed, step, 1)
            placed = jnp.where((shifts & step) != 0, moved, placed)
            step *= 2
        wide = jnp.concatenate([placed, jnp.zeros_like(placed)], axis=1)
        band = pltpu.roll(wide, taps // 2, 1, stride=1, stride_axis=0).astype(jnp.bfloat16)
        top = pl.multiple_of(b * BLK + BLK // 2, BLK // 2)
        moved = jnp.dot(
            band, compressed[pl.ds(top, PAIR), :], preferred_element_type=jnp.float32
        ).astype(jnp.bfloat16)
        bins = outgoing.shape[2]
        peers = BLK // bins
        first = b * peers
        for part in range(2):
            outgoing[pl.ds(first, peers), part] = moved[:, part * BLK : (part + 1) * BLK].reshape(
                peers, bins, BLK
            )

        def send(n, carry):
            peer = first + n

            @pl.when(peer != me)
            def _():
                pltpu.make_async_remote_copy(
                    src_ref=outgoing.at[peer],
                    dst_ref=gathered.at[me],
                    send_sem=send_sem,
                    recv_sem=recv_sem,
                    device_id=(peer, quarter),
                    device_id_type=MESH,
                ).start()

            return carry

        lax.fori_loop(0, peers, send, 0)

    compress(0)
    compress(1)

    def inner(j, carry):
        compress(j)
        migrate(j - 1)
        return carry

    inner_end = blocks - taps_blocks
    lax.fori_loop(2, inner_end, inner, 0)

    @pl.when(has_left)
    def _():
        to_right.wait_recv()

    @pl.when(has_right)
    def _():
        to_left.wait_recv()

    @pl.when(jnp.logical_not(has_right))
    def _():
        right_halo[...] = jnp.zeros_like(right_halo)

    join(right_halo, blocks + 1, reach // BLK)

    @pl.when(has_left)
    def _():
        join(left_halo, 0, 1)
        compress(-1)

    @pl.when(jnp.logical_not(has_left))
    def _():
        compressed[0:BLK, :] = jnp.zeros((BLK, PAIR), jnp.bfloat16)

    migrate(0)
    lax.fori_loop(inner_end, blocks + 1, inner, 0)

    keep = pltpu.make_async_copy(outgoing.at[me], gathered.at[me], local_sem)
    keep.start()
    place_toeplitz(azimuth_ref, azimuth_rows, azimuth_turned, azimuth_held)
    store = pltpu.make_async_copy(azimuth_held, azimuth_matrix, matrix_sem)
    store.start()

    @pl.when(has_left)
    def _():
        to_left.wait_send()

    @pl.when(has_right)
    def _():
        to_right.wait_send()

    keep.wait()
    store.wait()
    others = pl.ds(0, pulse_peers - 1)
    pltpu.make_async_copy(outgoing.at[others], gathered.at[others], send_sem).wait()
    pltpu.make_async_copy(outgoing.at[others], gathered.at[others], recv_sem).wait()


def focus_kernel(gathered, matrix, image, padded):
    step = pl.program_id(0)
    sources = gathered.shape[0]
    bins = gathered.shape[2]
    reach = matrix.shape[0] // PAIR
    edge = (reach - 1) // 2 * bins

    @pl.when(step == 0)
    def _():
        padded[0:edge, :] = jnp.zeros((edge, PAIR), jnp.bfloat16)
        padded[edge + sources * bins :, :] = jnp.zeros((edge, PAIR), jnp.bfloat16)
        for part in range(2):
            padded[edge : edge + sources * bins, part * BLK : (part + 1) * BLK] = gathered[
                :, part
            ].reshape(sources * bins, BLK)

    count = image.shape[3] // BLK
    top = pl.multiple_of(step * count * bins, bins)
    window = jnp.concatenate(
        [padded[pl.ds(pl.multiple_of(top + k * bins, bins), count * bins), :] for k in range(reach)],
        axis=1,
    )
    focused = jnp.dot(window, matrix[...], preferred_element_type=jnp.float32)
    for n in range(count):
        for part in range(2):
            image[part, 0, :, n * BLK : (n + 1) * BLK] = focused[
                n * bins : (n + 1) * bins, part * BLK : (part + 1) * BLK
            ]


def per_device(echoes, range_ref, band_weights, band_offsets, azimuth_ref):
    pulse_peers = lax.axis_size("pulse")
    quarters = lax.axis_size("rng")
    pulse_rows = echoes.shape[1]
    quarter_len = echoes.shape[2]
    blocks = quarter_len // BLK
    bins = quarter_len // pulse_peers
    range_blocks = range_ref.shape[1] // BLK
    azimuth_blocks = azimuth_ref.shape[1] // BLK
    reach = (range_blocks + 1) * BLK
    range_pad = -(-(2 * range_blocks + 2) // 8) * 8
    azimuth_pad = -(-(2 * azimuth_blocks + 2) // 8) * 8
    range_depth = (range_blocks + 1) * PAIR
    azimuth_depth = (azimuth_blocks + 1) * PAIR
    anywhere = pl.BlockSpec(memory_space=pl.ANY)
    in_vmem = pl.BlockSpec(memory_space=pltpu.VMEM)

    def kernel(*refs):
        compress_kernel(pulse_peers, quarters, *refs)

    gathered, matrix = pl.pallas_call(
        kernel,
        out_shape=(
            jax.ShapeDtypeStruct((pulse_peers, 2, bins, pulse_rows), jnp.bfloat16),
            jax.ShapeDtypeStruct((azimuth_depth, PAIR), jnp.bfloat16),
        ),
        in_specs=[anywhere, in_vmem, in_vmem, in_vmem, in_vmem],
        out_specs=(anywhere, anywhere),
        scratch_shapes=[
            pltpu.VMEM((2, pulse_rows, quarter_len), jnp.bfloat16),
            pltpu.VMEM((2, pulse_rows, reach), jnp.bfloat16),
            pltpu.VMEM((2, pulse_rows, BLK), jnp.bfloat16),
            pltpu.VMEM((pulse_rows, (blocks + 1 + reach // BLK) * PAIR), jnp.bfloat16),
            pltpu.VMEM((range_pad, PAIR), jnp.float32),
            pltpu.VMEM((range_pad, PAIR), jnp.float32),
            pltpu.VMEM((range_depth, PAIR), jnp.bfloat16),
            pltpu.VMEM((azimuth_pad, PAIR), jnp.float32),
            pltpu.VMEM((azimuth_pad, PAIR), jnp.float32),
            pltpu.VMEM((azimuth_depth, PAIR), jnp.bfloat16),
            pltpu.VMEM(((blocks + 2) * BLK, PAIR), jnp.bfloat16),
            pltpu.VMEM((pulse_peers, 2, bins, pulse_rows), jnp.bfloat16),
            pltpu.SemaphoreType.DMA,
            pltpu.SemaphoreType.DMA((2,)),
            pltpu.SemaphoreType.DMA((2,)),
            pltpu.SemaphoreType.DMA,
            pltpu.SemaphoreType.DMA,
            pltpu.SemaphoreType.DMA,
            pltpu.SemaphoreType.DMA,
        ],
        compiler_params=pltpu.CompilerParams(
            collective_id=0, has_side_effects=True, vmem_limit_bytes=VMEM_BYTES
        ),
        name="compress_and_exchange",
    )(echoes, range_ref, band_weights, band_offsets.reshape(blocks, BLK), azimuth_ref)

    steps = 8
    pulses = pulse_peers * pulse_rows
    return pl.pallas_call(
        focus_kernel,
        out_shape=jax.ShapeDtypeStruct((2, 1, bins, pulses), jnp.float32),
        grid=(steps,),
        in_specs=[
            pl.BlockSpec((pulse_peers, 2, bins, pulse_rows), lambda s: (0, 0, 0, 0)),
            pl.BlockSpec((azimuth_depth, PAIR), lambda s: (0, 0)),
        ],
        out_specs=pl.BlockSpec((2, 1, bins, pulses // steps), lambda s: (0, 0, 0, s)),
        scratch_shapes=[
            pltpu.VMEM(((pulse_peers + azimuth_blocks) * bins, PAIR), jnp.bfloat16)
        ],
        compiler_params=pltpu.CompilerParams(vmem_limit_bytes=VMEM_BYTES),
        name="focus",
    )(gathered, matrix)


def solution(mesh):
    return jax.shard_map(
        per_device,
        mesh=mesh,
        in_specs=(P(None, "pulse", "rng"), P(), P(None, "rng"), P("rng"), P()),
        out_specs=P(None, "rng", "pulse", None),
        check_vma=False,
    )
```

```python
import jax
import jax.numpy as jnp
from jax import lax
from jax.experimental import pallas as pl
from jax.experimental.pallas import tpu as pltpu
from jax.sharding import PartitionSpec as P

MESH = pl.DeviceIdType.MESH
BLK = 128
PAIR = 2 * BLK
VMEM_BYTES = 56 * 1024 * 1024


def place_toeplitz(taps_ref, rows_ref, turned_ref, matrix_ref):
    chunks = taps_ref.shape[1] // BLK
    rows_ref[...] = jnp.zeros_like(rows_ref)
    for k in range(chunks):
        chunk = taps_ref[:, k * BLK : (k + 1) * BLK].astype(jnp.float32)
        rows_ref[2 * k : 2 * k + 2, BLK:PAIR] = chunk
        rows_ref[2 * k + 2 : 2 * k + 4, 0:BLK] = chunk
    source = lax.broadcasted_iota(jnp.int32, (PAIR, PAIR), 0)
    lane = lax.broadcasted_iota(jnp.int32, (PAIR, PAIR), 1)
    wanted = jnp.where(lane < BLK, BLK - lane, 3 * BLK - lane)
    turn = jnp.where(source == wanted, 1.0, 0.0).astype(jnp.bfloat16)
    turned_ref[...] = jnp.dot(
        rows_ref[...].astype(jnp.bfloat16), turn, preferred_element_type=jnp.float32
    )
    for k in range(chunks + 1):
        tiles = []
        for part in range(2):
            row = turned_ref[2 * k + part : 2 * k + part + 1, :]
            spread = jnp.broadcast_to(row, (BLK, PAIR))
            tiles.append(pltpu.roll(spread, 0, 1, stride=1, stride_axis=0)[:, :BLK])
        real, imag = tiles
        top = k * PAIR
        matrix_ref[top : top + BLK, 0:BLK] = real.astype(jnp.bfloat16)
        matrix_ref[top : top + BLK, BLK:PAIR] = (-imag).astype(jnp.bfloat16)
        matrix_ref[top + BLK : top + PAIR, 0:BLK] = imag.astype(jnp.bfloat16)
        matrix_ref[top + BLK : top + PAIR, BLK:PAIR] = real.astype(jnp.bfloat16)


def focus_whole(
    pulse_peers,
    quarters,
    echoes_hbm,
    range_hbm,
    weights_hbm,
    offsets_hbm,
    azimuth_hbm,
    image,
    own,
    right_halo,
    left_halo,
    range_ref,
    weights,
    offsets,
    azimuth_ref,
    joined,
    range_rows,
    range_turned,
    range_matrix,
    azimuth_rows,
    azimuth_turned,
    azimuth_matrix,
    compressed,
    outgoing,
    gathered,
    focused,
    load_sem,
    halo_send_sem,
    halo_recv_sem,
    send_sem,
    recv_sem,
    local_sem,
    image_sem,
):
    me = lax.axis_index("pulse")
    quarter = lax.axis_index("rng")
    pulse_rows = own.shape[1]
    quarter_len = own.shape[2]
    blocks = quarter_len // BLK
    range_steps = range_matrix.shape[0] // PAIR
    azimuth_steps = azimuth_matrix.shape[0] // PAIR
    taps = weights.shape[0]
    bins = outgoing.shape[2]
    peers = BLK // bins
    groups = recv_sem.shape[0]
    group = pulse_peers // groups
    edge = (azimuth_steps - 1) // 2
    has_right = quarter < quarters - 1
    has_left = quarter > 0

    barrier = pltpu.get_barrier_semaphore()

    loads = [
        pltpu.make_async_copy(source, target, load_sem.at[n])
        for n, (source, target) in enumerate(
            (
                (range_hbm, range_ref),
                (echoes_hbm, own),
                (weights_hbm, weights),
                (offsets_hbm, offsets),
                (azimuth_hbm, azimuth_ref),
            )
        )
    ]
    for load in loads:
        load.start()

    @pl.when(has_right)
    def _():
        pl.semaphore_signal(barrier, inc=1, device_id=(me, quarter + 1), device_id_type=MESH)

    @pl.when(has_left)
    def _():
        pl.semaphore_signal(barrier, inc=1, device_id=(me, quarter - 1), device_id_type=MESH)

    def greet(step, carry):
        peer = lax.rem(me + step, pulse_peers)
        pl.semaphore_signal(barrier, inc=1, device_id=(peer, quarter), device_id_type=MESH)
        return carry

    lax.fori_loop(1, pulse_peers, greet, 0)

    loads[0].wait()
    place_toeplitz(range_ref, range_rows, range_turned, range_matrix)
    for load in loads[1:]:
        load.wait()

    def join(source, first, count):
        for m in range(count):
            for part in range(2):
                joined[
                    (first + m) * pulse_rows : (first + m + 1) * pulse_rows,
                    part * BLK : (part + 1) * BLK,
                ] = source[part, :, m * BLK : (m + 1) * BLK]

    join(own, 1, blocks)

    def compress(*js):
        window = jnp.concatenate(
            [
                jnp.concatenate(
                    [
                        joined[
                            pl.ds(pl.multiple_of((j + 1 + k) * pulse_rows, pulse_rows), pulse_rows)
                        ]
                        for j in js
                    ],
                    axis=0,
                )
                for k in range(range_steps)
            ],
            axis=1,
        )
        block = jnp.dot(window, range_matrix[...], preferred_element_type=jnp.float32)
        block = block.astype(jnp.bfloat16)
        for n, j in enumerate(js):
            at = pl.ds(pl.multiple_of((j + 1) * BLK, BLK), BLK)
            for part in range(2):
                compressed[part * pulse_rows : (part + 1) * pulse_rows, at] = block[
                    n * pulse_rows : (n + 1) * pulse_rows, part * BLK : (part + 1) * BLK
                ]

    def band_of(b):
        start = BLK - BLK // 2 + taps // 2
        lane = lax.broadcasted_iota(jnp.int32, (8, BLK), 1)
        shift = jnp.broadcast_to(offsets[pl.ds(b, 1), :], (8, BLK)) + lane

        def shifted(bit, rows):
            return jnp.concatenate([(shift & bit) != 0] * (rows // 8), axis=0)

        table = weights[:, pl.ds(pl.multiple_of(b * BLK, BLK), BLK)].astype(jnp.float32)
        placed = jnp.concatenate([table, jnp.zeros((8, BLK), jnp.float32)], axis=0)
        for bit in (1, 2, 4):
            rows = placed.shape[0]
            placed = jnp.where(shifted(bit, rows), pltpu.roll(placed, bit, 0), placed)
        bit = 8
        while bit <= BLK - 1 + taps // 2:
            blank = jnp.zeros((bit, BLK), jnp.float32)
            lower = jnp.concatenate([blank, placed], axis=0)
            upper = jnp.concatenate([placed, blank], axis=0)
            placed = jnp.where(shifted(bit, lower.shape[0]), lower, upper)
            bit *= 2
        return jnp.concatenate(
            [jnp.zeros((start, BLK), jnp.float32), placed[: 3 * BLK - start]], axis=0
        ).astype(jnp.bfloat16)

    def migrate(b):
        around = compressed[:, pl.ds(pl.multiple_of(b * BLK, BLK), 3 * BLK)]
        moved = jnp.dot(around, band_of(b), preferred_element_type=jnp.float32)
        for part in range(2):
            turned = moved[part * pulse_rows : (part + 1) * pulse_rows].T.astype(jnp.bfloat16)
            outgoing[pl.ds(b * peers, peers), part] = turned.reshape(peers, bins, pulse_rows)

    def send(b):
        def one(n, carry):
            peer = b * peers + n

            @pl.when(peer != me)
            def _():
                pltpu.make_async_remote_copy(
                    src_ref=outgoing.at[peer],
                    dst_ref=gathered.at[me + edge],
                    send_sem=send_sem,
                    recv_sem=recv_sem.at[me // group],
                    device_id=(peer, quarter),
                    device_id_type=MESH,
                ).start()

            return carry

        lax.fori_loop(0, peers, one, 0)

    half = blocks - range_steps + 1
    compress(0, 1)

    def first_pairs(i, carry):
        compress(2 * i, 2 * i + 1)
        migrate(2 * i - 1)
        migrate(2 * i)
        return carry

    lax.fori_loop(1, half // 2, first_pairs, 0)

    neighbours = jnp.where(has_right, 1, 0) + jnp.where(has_left, 1, 0)
    pl.semaphore_wait(barrier, pulse_peers - 1 + neighbours)

    reach = right_halo.shape[2]
    to_left = pltpu.make_async_remote_copy(
        src_ref=own.at[:, :, pl.ds(0, reach)],
        dst_ref=right_halo,
        send_sem=halo_send_sem.at[0],
        recv_sem=halo_recv_sem.at[0],
        device_id=(me, quarter - 1),
        device_id_type=MESH,
    )
    to_right = pltpu.make_async_remote_copy(
        src_ref=own.at[:, :, pl.ds(quarter_len - BLK, BLK)],
        dst_ref=left_halo,
        send_sem=halo_send_sem.at[1],
        recv_sem=halo_recv_sem.at[1],
        device_id=(me, quarter + 1),
        device_id_type=MESH,
    )

    @pl.when(has_left)
    def _():
        to_left.start()

    @pl.when(has_right)
    def _():
        to_right.start()

    def send_first(b, carry):
        send(b)
        return carry

    lax.fori_loop(1, half - 1, send_first, 0)

    place_toeplitz(azimuth_ref, azimuth_rows, azimuth_turned, azimuth_matrix)
    gathered[0:edge] = jnp.zeros((edge,) + gathered.shape[1:], jnp.bfloat16)
    gathered[edge + pulse_peers :] = jnp.zeros((edge,) + gathered.shape[1:], jnp.bfloat16)

    @pl.when(has_left)
    def _():
        to_right.wait_recv()
        join(left_halo, 0, 1)

    @pl.when(has_right)
    def _():
        to_left.wait_recv()
        join(right_halo, blocks + 1, reach // BLK)

    @pl.when(jnp.logical_not(has_left))
    def _():
        joined[0:pulse_rows, :] = jnp.zeros((pulse_rows, PAIR), jnp.bfloat16)

    @pl.when(jnp.logical_not(has_right))
    def _():
        rest = reach // BLK * pulse_rows
        joined[(blocks + 1) * pulse_rows :, :] = jnp.zeros((rest, PAIR), jnp.bfloat16)

    compress(-1, half)

    @pl.when(jnp.logical_not(has_left))
    def _():
        compressed[:, 0:BLK] = jnp.zeros((2 * pulse_rows, BLK), jnp.bfloat16)

    migrate(0)
    send(0)
    migrate(half - 1)
    send(half - 1)

    def second_pairs(i, carry):
        j = half + 1 + 2 * i
        compress(j, j + 1)
        migrate(j - 1)
        send(j - 1)
        migrate(j)
        send(j)
        return carry

    lax.fori_loop(0, (blocks - half) // 2, second_pairs, 0)

    keep = pltpu.make_async_copy(outgoing.at[me], gathered.at[me + edge], local_sem)
    keep.start()
    keep.wait()

    def arrive(g):
        for count, mine in ((group - 1, True), (group, False)):

            @pl.when((me // group == g) == mine)
            def _():
                pltpu.make_async_copy(
                    outgoing.at[pl.ds(0, count)], gathered.at[pl.ds(edge, count)], recv_sem.at[g]
                ).wait()

    def put(g):
        lanes = pl.ds(pl.multiple_of(g * group * BLK, BLK), group * BLK)
        return pltpu.make_async_copy(
            focused.at[:, :, :, lanes], image.at[:, :, :, lanes], image_sem
        )

    def focus(g, carry):
        @pl.when(g < groups - 1)
        def _():
            arrive(g + 1)

        window = jnp.concatenate(
            [
                gathered[pl.ds(g * group + k, group), part].reshape(group * bins, pulse_rows)
                for k in range(azimuth_steps)
                for part in range(2)
            ],
            axis=1,
        )
        result = jnp.dot(window, azimuth_matrix[...], preferred_element_type=jnp.float32)
        for n in range(group):
            at = pl.ds(pl.multiple_of((g * group + n) * BLK, BLK), BLK)
            for part in range(2):
                focused[part, 0, :, at] = result[
                    n * bins : (n + 1) * bins, part * BLK : (part + 1) * BLK
                ]
        put(g).start()
        return carry

    arrive(0)
    lax.fori_loop(0, groups, focus, 0)

    @pl.when(has_left)
    def _():
        to_left.wait_send()

    @pl.when(has_right)
    def _():
        to_right.wait_send()

    others = pl.ds(0, pulse_peers - 1)
    pltpu.make_async_copy(outgoing.at[others], gathered.at[others], send_sem).wait()
    pltpu.make_async_copy(focused, image, image_sem).wait()


def place_image(source, image, held, load_sem, store_sem):
    count = load_sem.shape[0]
    width = image.shape[3] // count
    stores = []
    loads = []
    for n in range(count):
        lanes = pl.ds(n * width, width)
        load = pltpu.make_async_copy(
            source.at[:, :, :, lanes], held.at[:, :, :, lanes], load_sem.at[n]
        )
        load.start()
        loads.append(load)
    for n in range(count):
        lanes = pl.ds(n * width, width)
        loads[n].wait()
        store = pltpu.make_async_copy(
            held.at[:, :, :, lanes], image.at[:, :, :, lanes], store_sem.at[n]
        )
        store.start()
        stores.append(store)
    for store in stores:
        store.wait()


def per_device(echoes, range_ref, band_weights, band_offsets, azimuth_ref):
    pulse_peers = lax.axis_size("pulse")
    quarters = lax.axis_size("rng")
    pulse_rows = echoes.shape[1]
    quarter_len = echoes.shape[2]
    blocks = quarter_len // BLK
    bins = quarter_len // pulse_peers
    range_blocks = range_ref.shape[1] // BLK
    azimuth_blocks = azimuth_ref.shape[1] // BLK
    reach = (range_blocks + 1) * BLK
    range_pad = -(-(2 * range_blocks + 2) // 8) * 8
    azimuth_pad = -(-(2 * azimuth_blocks + 2) // 8) * 8
    range_depth = (range_blocks + 1) * PAIR
    azimuth_depth = (azimuth_blocks + 1) * PAIR
    pulses = pulse_peers * pulse_rows
    groups = 16
    anywhere = pl.BlockSpec(memory_space=pl.ANY)
    bf16 = jnp.bfloat16
    f32 = jnp.float32
    image_shape = (2, 1, bins, pulses)

    def kernel(*refs):
        focus_whole(pulse_peers, quarters, *refs)

    image = pl.pallas_call(
        kernel,
        out_shape=jax.ShapeDtypeStruct(image_shape, f32),
        in_specs=[anywhere] * 5,
        out_specs=anywhere,
        scratch_shapes=[
            pltpu.VMEM((2, pulse_rows, quarter_len), bf16),
            pltpu.VMEM((2, pulse_rows, reach), bf16),
            pltpu.VMEM((2, pulse_rows, BLK), bf16),
            pltpu.VMEM(range_ref.shape, bf16),
            pltpu.VMEM(band_weights.shape, bf16),
            pltpu.VMEM((blocks, BLK), jnp.int32),
            pltpu.VMEM(azimuth_ref.shape, bf16),
            pltpu.VMEM(((blocks + 1 + reach // BLK) * pulse_rows, PAIR), bf16),
            pltpu.VMEM((range_pad, PAIR), f32),
            pltpu.VMEM((range_pad, PAIR), f32),
            pltpu.VMEM((range_depth, PAIR), bf16),
            pltpu.VMEM((azimuth_pad, PAIR), f32),
            pltpu.VMEM((azimuth_pad, PAIR), f32),
            pltpu.VMEM((azimuth_depth, PAIR), bf16),
            pltpu.VMEM((2 * pulse_rows, (blocks + 2) * BLK), bf16),
            pltpu.VMEM((pulse_peers, 2, bins, pulse_rows), bf16),
            pltpu.VMEM((pulse_peers + azimuth_blocks, 2, bins, pulse_rows), bf16),
            pltpu.VMEM(image_shape, f32),
            pltpu.SemaphoreType.DMA((5,)),
            pltpu.SemaphoreType.DMA((2,)),
            pltpu.SemaphoreType.DMA((2,)),
            pltpu.SemaphoreType.DMA,
            pltpu.SemaphoreType.DMA((groups,)),
            pltpu.SemaphoreType.DMA,
            pltpu.SemaphoreType.DMA,
        ],
        compiler_params=pltpu.CompilerParams(
            collective_id=0, has_side_effects=True, vmem_limit_bytes=VMEM_BYTES
        ),
        name="focus_whole",
    )(echoes, range_ref, band_weights, band_offsets.reshape(blocks, BLK), azimuth_ref)

    pieces = 4
    return pl.pallas_call(
        place_image,
        out_shape=jax.ShapeDtypeStruct(image_shape, f32),
        in_specs=[anywhere],
        out_specs=anywhere,
        scratch_shapes=[
            pltpu.VMEM(image_shape, f32),
            pltpu.SemaphoreType.DMA((pieces,)),
            pltpu.SemaphoreType.DMA((pieces,)),
        ],
        compiler_params=pltpu.CompilerParams(vmem_limit_bytes=VMEM_BYTES),
        name="place_image",
    )(image)


def solution(mesh):
    return jax.shard_map(
        per_device,
        mesh=mesh,
        in_specs=(P(None, "pulse", "rng"), P(), P(None, "rng"), P("rng"), P()),
        out_specs=P(None, "rng", "pulse", None),
        check_vma=False,
    )
```

```python
import jax
import jax.numpy as jnp
from jax import lax
from jax.experimental import pallas as pl
from jax.experimental.pallas import tpu as pltpu
from jax.sharding import PartitionSpec as P

MESH = pl.DeviceIdType.MESH
BLK = 128
PAIR = 2 * BLK
VMEM_BYTES = 44 * 1024 * 1024


def place_toeplitz(taps_ref, rows_ref, turned_ref, matrix_ref):
    chunks = taps_ref.shape[1] // BLK
    rows_ref[...] = jnp.zeros_like(rows_ref)
    for k in range(chunks):
        chunk = taps_ref[:, k * BLK : (k + 1) * BLK].astype(jnp.float32)
        rows_ref[2 * k : 2 * k + 2, BLK:PAIR] = chunk
        rows_ref[2 * k + 2 : 2 * k + 4, 0:BLK] = chunk
    source = lax.broadcasted_iota(jnp.int32, (PAIR, PAIR), 0)
    lane = lax.broadcasted_iota(jnp.int32, (PAIR, PAIR), 1)
    wanted = jnp.where(lane < BLK, BLK - lane, 3 * BLK - lane)
    turn = jnp.where(source == wanted, 1.0, 0.0).astype(jnp.bfloat16)
    turned_ref[...] = jnp.dot(
        rows_ref[...].astype(jnp.bfloat16), turn, preferred_element_type=jnp.float32
    )
    for k in range(chunks + 1):
        tiles = []
        for part in range(2):
            row = turned_ref[2 * k + part : 2 * k + part + 1, :]
            spread = jnp.broadcast_to(row, (BLK, PAIR))
            tiles.append(pltpu.roll(spread, 0, 1, stride=1, stride_axis=0)[:, :BLK])
        real, imag = tiles
        top = k * PAIR
        matrix_ref[top : top + BLK, 0:BLK] = real.astype(jnp.bfloat16)
        matrix_ref[top : top + BLK, BLK:PAIR] = (-imag).astype(jnp.bfloat16)
        matrix_ref[top + BLK : top + PAIR, 0:BLK] = imag.astype(jnp.bfloat16)
        matrix_ref[top + BLK : top + PAIR, BLK:PAIR] = real.astype(jnp.bfloat16)


def focus_whole(
    pulse_peers,
    quarters,
    echoes_hbm,
    range_hbm,
    weights_hbm,
    offsets_hbm,
    azimuth_hbm,
    image,
    own,
    right_halo,
    left_halo,
    range_ref,
    weights,
    offsets,
    azimuth_ref,
    joined,
    range_rows,
    range_turned,
    range_matrix,
    azimuth_rows,
    azimuth_turned,
    azimuth_matrix,
    compressed,
    outgoing,
    gathered,
    load_sem,
    halo_send_sem,
    halo_recv_sem,
    send_sem,
    recv_sem,
    local_sem,
):
    me = lax.axis_index("pulse")
    quarter = lax.axis_index("rng")
    pulse_rows = own.shape[1]
    quarter_len = own.shape[2]
    blocks = quarter_len // BLK
    range_steps = range_matrix.shape[0] // PAIR
    azimuth_steps = azimuth_matrix.shape[0] // PAIR
    taps = weights.shape[0]
    bins = outgoing.shape[2]
    peers = BLK // bins
    groups = recv_sem.shape[0]
    group = pulse_peers // groups
    edge = (azimuth_steps - 1) // 2
    has_right = quarter < quarters - 1
    has_left = quarter > 0

    barrier = pltpu.get_barrier_semaphore()

    loads = [
        pltpu.make_async_copy(source, target, load_sem.at[n])
        for n, (source, target) in enumerate(
            (
                (range_hbm, range_ref),
                (echoes_hbm, own),
                (weights_hbm, weights),
                (offsets_hbm, offsets),
                (azimuth_hbm, azimuth_ref),
            )
        )
    ]
    for load in loads:
        load.start()

    @pl.when(has_right)
    def _():
        pl.semaphore_signal(barrier, inc=1, device_id=(me, quarter + 1), device_id_type=MESH)

    @pl.when(has_left)
    def _():
        pl.semaphore_signal(barrier, inc=1, device_id=(me, quarter - 1), device_id_type=MESH)

    def greet(step, carry):
        peer = lax.rem(me + step, pulse_peers)
        pl.semaphore_signal(barrier, inc=1, device_id=(peer, quarter), device_id_type=MESH)
        return carry

    lax.fori_loop(1, pulse_peers, greet, 0)

    loads[0].wait()
    place_toeplitz(range_ref, range_rows, range_turned, range_matrix)
    for load in loads[1:]:
        load.wait()

    def join(source, first, count):
        for m in range(count):
            for part in range(2):
                joined[
                    (first + m) * pulse_rows : (first + m + 1) * pulse_rows,
                    part * BLK : (part + 1) * BLK,
                ] = source[part, :, m * BLK : (m + 1) * BLK]

    join(own, 1, blocks)

    def compress(*js):
        window = jnp.concatenate(
            [
                jnp.concatenate(
                    [
                        joined[
                            pl.ds(pl.multiple_of((j + 1 + k) * pulse_rows, pulse_rows), pulse_rows)
                        ]
                        for j in js
                    ],
                    axis=0,
                )
                for k in range(range_steps)
            ],
            axis=1,
        )
        block = jnp.dot(window, range_matrix[...], preferred_element_type=jnp.float32)
        block = block.astype(jnp.bfloat16)
        for n, j in enumerate(js):
            at = pl.ds(pl.multiple_of((j + 1) * BLK, BLK), BLK)
            for part in range(2):
                compressed[part * pulse_rows : (part + 1) * pulse_rows, at] = block[
                    n * pulse_rows : (n + 1) * pulse_rows, part * BLK : (part + 1) * BLK
                ]

    def band_of(b):
        start = BLK - BLK // 2 + taps // 2
        lane = lax.broadcasted_iota(jnp.int32, (8, BLK), 1)
        shift = jnp.broadcast_to(offsets[pl.ds(b, 1), :], (8, BLK)) + lane

        def shifted(bit, rows):
            return jnp.concatenate([(shift & bit) != 0] * (rows // 8), axis=0)

        table = weights[:, pl.ds(pl.multiple_of(b * BLK, BLK), BLK)].astype(jnp.float32)
        placed = jnp.concatenate([table, jnp.zeros((8, BLK), jnp.float32)], axis=0)
        for bit in (1, 2, 4):
            rows = placed.shape[0]
            placed = jnp.where(shifted(bit, rows), pltpu.roll(placed, bit, 0), placed)
        bit = 8
        while bit <= BLK - 1 + taps // 2:
            blank = jnp.zeros((bit, BLK), jnp.float32)
            lower = jnp.concatenate([blank, placed], axis=0)
            upper = jnp.concatenate([placed, blank], axis=0)
            placed = jnp.where(shifted(bit, lower.shape[0]), lower, upper)
            bit *= 2
        return jnp.concatenate(
            [jnp.zeros((start, BLK), jnp.float32), placed[: 3 * BLK - start]], axis=0
        ).astype(jnp.bfloat16)

    def migrate(b):
        around = compressed[:, pl.ds(pl.multiple_of(b * BLK, BLK), 3 * BLK)]
        moved = jnp.dot(around, band_of(b), preferred_element_type=jnp.float32)
        for part in range(2):
            turned = moved[part * pulse_rows : (part + 1) * pulse_rows].T.astype(jnp.bfloat16)
            outgoing[pl.ds(b * peers, peers), part] = turned.reshape(peers, bins, pulse_rows)

    def send(b):
        def one(n, carry):
            peer = b * peers + n

            @pl.when(peer != me)
            def _():
                pltpu.make_async_remote_copy(
                    src_ref=outgoing.at[peer],
                    dst_ref=gathered.at[me + edge],
                    send_sem=send_sem,
                    recv_sem=recv_sem.at[me // group],
                    device_id=(peer, quarter),
                    device_id_type=MESH,
                ).start()

            return carry

        lax.fori_loop(0, peers, one, 0)

    half = blocks - range_steps + 1
    compress(0, 1)

    def first_pairs(i, carry):
        compress(2 * i, 2 * i + 1)
        migrate(2 * i - 1)
        migrate(2 * i)
        return carry

    lax.fori_loop(1, half // 2, first_pairs, 0)

    neighbours = jnp.where(has_right, 1, 0) + jnp.where(has_left, 1, 0)
    pl.semaphore_wait(barrier, pulse_peers - 1 + neighbours)

    reach = right_halo.shape[2]
    to_left = pltpu.make_async_remote_copy(
        src_ref=own.at[:, :, pl.ds(0, reach)],
        dst_ref=right_halo,
        send_sem=halo_send_sem.at[0],
        recv_sem=halo_recv_sem.at[0],
        device_id=(me, quarter - 1),
        device_id_type=MESH,
    )
    to_right = pltpu.make_async_remote_copy(
        src_ref=own.at[:, :, pl.ds(quarter_len - BLK, BLK)],
        dst_ref=left_halo,
        send_sem=halo_send_sem.at[1],
        recv_sem=halo_recv_sem.at[1],
        device_id=(me, quarter + 1),
        device_id_type=MESH,
    )

    @pl.when(has_left)
    def _():
        to_left.start()

    @pl.when(has_right)
    def _():
        to_right.start()

    stride = blocks // 4
    send(stride)

    def send_first(b, carry):
        send(b)
        return carry

    lax.fori_loop(1, stride, send_first, 0)

    place_toeplitz(azimuth_ref, azimuth_rows, azimuth_turned, azimuth_matrix)
    gathered[0:edge] = jnp.zeros((edge,) + gathered.shape[1:], jnp.bfloat16)
    gathered[edge + pulse_peers :] = jnp.zeros((edge,) + gathered.shape[1:], jnp.bfloat16)

    @pl.when(has_left)
    def _():
        to_right.wait_recv()
        join(left_halo, 0, 1)

    @pl.when(has_right)
    def _():
        to_left.wait_recv()
        join(right_halo, blocks + 1, reach // BLK)

    @pl.when(jnp.logical_not(has_left))
    def _():
        joined[0:pulse_rows, :] = jnp.zeros((pulse_rows, PAIR), jnp.bfloat16)

    @pl.when(jnp.logical_not(has_right))
    def _():
        rest = reach // BLK * pulse_rows
        joined[(blocks + 1) * pulse_rows :, :] = jnp.zeros((rest, PAIR), jnp.bfloat16)

    compress(-1, half)

    @pl.when(jnp.logical_not(has_left))
    def _():
        compressed[:, 0:BLK] = jnp.zeros((2 * pulse_rows, BLK), jnp.bfloat16)

    migrate(0)
    send(0)

    def second_pairs(i, carry):
        j = half + 1 + 2 * i
        compress(j, j + 1)
        return carry

    lax.fori_loop(0, (blocks - half) // 2, second_pairs, 0)

    def late(u, carry):
        b = half + u // 2 + stride * (u % 2)
        migrate(b)
        send(b)
        return carry

    lax.fori_loop(0, 2, late, 0)
    lax.fori_loop(stride + 1, half - 1, send_first, 0)
    lax.fori_loop(2, 6, late, 0)
    migrate(half - 1)
    send(half - 1)
    lax.fori_loop(6, 8, late, 0)

    keep = pltpu.make_async_copy(outgoing.at[me], gathered.at[me + edge], local_sem)
    keep.start()
    keep.wait()

    def arrive(g):
        for count, mine in ((group - 1, True), (group, False)):

            @pl.when((me // group == g) == mine)
            def _():
                pltpu.make_async_copy(
                    outgoing.at[pl.ds(0, count)], gathered.at[pl.ds(edge, count)], recv_sem.at[g]
                ).wait()

    def focus(g, carry):
        @pl.when(g < groups - 1)
        def _():
            arrive(g + 1)

        window = jnp.concatenate(
            [
                gathered[pl.ds(g * group + k, group), part].reshape(group * bins, pulse_rows)
                for k in range(azimuth_steps)
                for part in range(2)
            ],
            axis=1,
        )
        result = jnp.dot(window, azimuth_matrix[...], preferred_element_type=jnp.float32)
        for n in range(group):
            at = pl.ds(pl.multiple_of((g * group + n) * BLK, BLK), BLK)
            for part in range(2):
                image[part, 0, :, at] = result[
                    n * bins : (n + 1) * bins, part * BLK : (part + 1) * BLK
                ]
        return carry

    arrive(0)
    lax.fori_loop(0, groups, focus, 0)

    @pl.when(has_left)
    def _():
        to_left.wait_send()

    @pl.when(has_right)
    def _():
        to_right.wait_send()

    others = pl.ds(0, pulse_peers - 1)
    pltpu.make_async_copy(outgoing.at[others], gathered.at[others], send_sem).wait()


def place_image(source, image, sem):
    copy = pltpu.make_async_copy(source, image, sem)
    copy.start()
    copy.wait()


def per_device(echoes, range_ref, band_weights, band_offsets, azimuth_ref):
    pulse_peers = lax.axis_size("pulse")
    quarters = lax.axis_size("rng")
    pulse_rows = echoes.shape[1]
    quarter_len = echoes.shape[2]
    blocks = quarter_len // BLK
    bins = quarter_len // pulse_peers
    range_blocks = range_ref.shape[1] // BLK
    azimuth_blocks = azimuth_ref.shape[1] // BLK
    reach = (range_blocks + 1) * BLK
    range_pad = -(-(2 * range_blocks + 2) // 8) * 8
    azimuth_pad = -(-(2 * azimuth_blocks + 2) // 8) * 8
    range_depth = (range_blocks + 1) * PAIR
    azimuth_depth = (azimuth_blocks + 1) * PAIR
    pulses = pulse_peers * pulse_rows
    groups = 8
    anywhere = pl.BlockSpec(memory_space=pl.ANY)
    in_vmem = pl.BlockSpec(memory_space=pltpu.VMEM)
    bf16 = jnp.bfloat16
    f32 = jnp.float32
    image_shape = (2, 1, bins, pulses)

    def kernel(*refs):
        focus_whole(pulse_peers, quarters, *refs)

    image = pl.pallas_call(
        kernel,
        out_shape=jax.ShapeDtypeStruct(image_shape, f32),
        in_specs=[anywhere] * 5,
        out_specs=in_vmem,
        scratch_shapes=[
            pltpu.VMEM((2, pulse_rows, quarter_len), bf16),
            pltpu.VMEM((2, pulse_rows, reach), bf16),
            pltpu.VMEM((2, pulse_rows, BLK), bf16),
            pltpu.VMEM(range_ref.shape, bf16),
            pltpu.VMEM(band_weights.shape, bf16),
            pltpu.VMEM((blocks, BLK), jnp.int32),
            pltpu.VMEM(azimuth_ref.shape, bf16),
            pltpu.VMEM(((blocks + 1 + reach // BLK) * pulse_rows, PAIR), bf16),
            pltpu.VMEM((range_pad, PAIR), f32),
            pltpu.VMEM((range_pad, PAIR), f32),
            pltpu.VMEM((range_depth, PAIR), bf16),
            pltpu.VMEM((azimuth_pad, PAIR), f32),
            pltpu.VMEM((azimuth_pad, PAIR), f32),
            pltpu.VMEM((azimuth_depth, PAIR), bf16),
            pltpu.VMEM((2 * pulse_rows, (blocks + 2) * BLK), bf16),
            pltpu.VMEM((pulse_peers, 2, bins, pulse_rows), bf16),
            pltpu.VMEM((pulse_peers + azimuth_blocks, 2, bins, pulse_rows), bf16),
            pltpu.SemaphoreType.DMA((5,)),
            pltpu.SemaphoreType.DMA((2,)),
            pltpu.SemaphoreType.DMA((2,)),
            pltpu.SemaphoreType.DMA,
            pltpu.SemaphoreType.DMA((groups,)),
            pltpu.SemaphoreType.DMA,
        ],
        compiler_params=pltpu.CompilerParams(
            collective_id=0, has_side_effects=True, vmem_limit_bytes=VMEM_BYTES
        ),
        name="focus_whole",
    )(
        *(
            pltpu.with_memory_space_constraint(operand, pltpu.HBM)
            for operand in (
                echoes,
                range_ref,
                band_weights,
                band_offsets.reshape(blocks, BLK),
                azimuth_ref,
            )
        )
    )

    return pl.pallas_call(
        place_image,
        out_shape=jax.ShapeDtypeStruct(image_shape, f32),
        in_specs=[in_vmem],
        out_specs=anywhere,
        scratch_shapes=[pltpu.SemaphoreType.DMA],
        compiler_params=pltpu.CompilerParams(vmem_limit_bytes=VMEM_BYTES),
        name="place_image",
    )(image)


def solution(mesh):
    return jax.shard_map(
        per_device,
        mesh=mesh,
        in_specs=(P(None, "pulse", "rng"), P(), P(None, "rng"), P("rng"), P()),
        out_specs=P(None, "rng", "pulse", None),
        check_vma=False,
    )
```

```python
import jax
import jax.numpy as jnp
from jax import lax
from jax.experimental import pallas as pl
from jax.experimental.pallas import tpu as pltpu
from jax.sharding import PartitionSpec as P

MESH = pl.DeviceIdType.MESH
BLK = 128
PAIR = 2 * BLK
VMEM_BYTES = 44 * 1024 * 1024


def place_toeplitz(taps_ref, rows_ref, turned_ref, matrix_ref):
    chunks = taps_ref.shape[1] // BLK
    rows_ref[...] = jnp.zeros_like(rows_ref)
    for k in range(chunks):
        chunk = taps_ref[:, k * BLK : (k + 1) * BLK].astype(jnp.float32)
        rows_ref[2 * k : 2 * k + 2, BLK:PAIR] = chunk
        rows_ref[2 * k + 2 : 2 * k + 4, 0:BLK] = chunk
    source = lax.broadcasted_iota(jnp.int32, (PAIR, PAIR), 0)
    lane = lax.broadcasted_iota(jnp.int32, (PAIR, PAIR), 1)
    wanted = jnp.where(lane < BLK, BLK - lane, 3 * BLK - lane)
    turn = jnp.where(source == wanted, 1.0, 0.0).astype(jnp.bfloat16)
    turned_ref[...] = jnp.dot(
        rows_ref[...].astype(jnp.bfloat16), turn, preferred_element_type=jnp.float32
    )
    for k in range(chunks + 1):
        tiles = []
        for part in range(2):
            row = turned_ref[2 * k + part : 2 * k + part + 1, :]
            spread = jnp.broadcast_to(row, (BLK, PAIR))
            tiles.append(pltpu.roll(spread, 0, 1, stride=1, stride_axis=0)[:, :BLK])
        real, imag = tiles
        top = k * PAIR
        matrix_ref[top : top + BLK, 0:BLK] = real.astype(jnp.bfloat16)
        matrix_ref[top : top + BLK, BLK:PAIR] = (-imag).astype(jnp.bfloat16)
        matrix_ref[top + BLK : top + PAIR, 0:BLK] = imag.astype(jnp.bfloat16)
        matrix_ref[top + BLK : top + PAIR, BLK:PAIR] = real.astype(jnp.bfloat16)


def focus_whole(
    pulse_peers,
    quarters,
    echoes_hbm,
    range_hbm,
    weights_hbm,
    offsets_hbm,
    azimuth_hbm,
    image,
    own,
    right_halo,
    left_halo,
    range_ref,
    weights,
    offsets,
    azimuth_ref,
    joined,
    range_rows,
    range_turned,
    range_matrix,
    azimuth_rows,
    azimuth_turned,
    azimuth_matrix,
    compressed,
    outgoing,
    gathered,
    load_sem,
    halo_send_sem,
    halo_recv_sem,
    send_sem,
    recv_sem,
    local_sem,
):
    me = lax.axis_index("pulse")
    quarter = lax.axis_index("rng")
    pulse_rows = own.shape[1]
    quarter_len = own.shape[2]
    blocks = quarter_len // BLK
    range_steps = range_matrix.shape[0] // PAIR
    azimuth_steps = azimuth_matrix.shape[0] // PAIR
    taps = weights.shape[0]
    bins = outgoing.shape[2]
    peers = BLK // bins
    groups = recv_sem.shape[0]
    group = pulse_peers // groups
    edge = (azimuth_steps - 1) // 2
    has_right = quarter < quarters - 1
    has_left = quarter > 0

    barrier = pltpu.get_barrier_semaphore()

    loads = [
        pltpu.make_async_copy(source, target, load_sem.at[n])
        for n, (source, target) in enumerate(
            (
                (range_hbm, range_ref),
                (echoes_hbm, own),
                (weights_hbm, weights),
                (offsets_hbm, offsets),
                (azimuth_hbm, azimuth_ref),
            )
        )
    ]
    for load in loads:
        load.start()

    @pl.when(has_right)
    def _():
        pl.semaphore_signal(barrier, inc=1, device_id=(me, quarter + 1), device_id_type=MESH)

    @pl.when(has_left)
    def _():
        pl.semaphore_signal(barrier, inc=1, device_id=(me, quarter - 1), device_id_type=MESH)

    def greet(step, carry):
        peer = lax.rem(me + step, pulse_peers)
        pl.semaphore_signal(barrier, inc=1, device_id=(peer, quarter), device_id_type=MESH)
        return carry

    lax.fori_loop(1, pulse_peers, greet, 0)

    loads[0].wait()
    place_toeplitz(range_ref, range_rows, range_turned, range_matrix)
    for load in loads[1:]:
        load.wait()

    def join(source, first, count):
        for m in range(count):
            for part in range(2):
                joined[
                    (first + m) * pulse_rows : (first + m + 1) * pulse_rows,
                    part * BLK : (part + 1) * BLK,
                ] = source[part, :, m * BLK : (m + 1) * BLK]

    join(own, 1, blocks)

    def compress(*js):
        window = jnp.concatenate(
            [
                jnp.concatenate(
                    [
                        joined[
                            pl.ds(pl.multiple_of((j + 1 + k) * pulse_rows, pulse_rows), pulse_rows)
                        ]
                        for j in js
                    ],
                    axis=0,
                )
                for k in range(range_steps)
            ],
            axis=1,
        )
        block = jnp.dot(window, range_matrix[...], preferred_element_type=jnp.float32)
        block = block.astype(jnp.bfloat16)
        for n, j in enumerate(js):
            at = pl.ds(pl.multiple_of((j + 1) * BLK, BLK), BLK)
            for part in range(2):
                compressed[part * pulse_rows : (part + 1) * pulse_rows, at] = block[
                    n * pulse_rows : (n + 1) * pulse_rows, part * BLK : (part + 1) * BLK
                ]

    def band_of(b):
        start = BLK - BLK // 2 + taps // 2
        lane = lax.broadcasted_iota(jnp.int32, (8, BLK), 1)
        shift = jnp.broadcast_to(offsets[pl.ds(b, 1), :], (8, BLK)) + lane

        def shifted(bit, rows):
            return jnp.concatenate([(shift & bit) != 0] * (rows // 8), axis=0)

        table = weights[:, pl.ds(pl.multiple_of(b * BLK, BLK), BLK)].astype(jnp.float32)
        placed = jnp.concatenate([table, jnp.zeros((8, BLK), jnp.float32)], axis=0)
        for bit in (1, 2, 4):
            rows = placed.shape[0]
            placed = jnp.where(shifted(bit, rows), pltpu.roll(placed, bit, 0), placed)
        bit = 8
        while bit <= BLK - 1 + taps // 2:
            blank = jnp.zeros((bit, BLK), jnp.float32)
            lower = jnp.concatenate([blank, placed], axis=0)
            upper = jnp.concatenate([placed, blank], axis=0)
            placed = jnp.where(shifted(bit, lower.shape[0]), lower, upper)
            bit *= 2
        return jnp.concatenate(
            [jnp.zeros((start, BLK), jnp.float32), placed[: 3 * BLK - start]], axis=0
        ).astype(jnp.bfloat16)

    def migrate(b):
        around = compressed[:, pl.ds(pl.multiple_of(b * BLK, BLK), 3 * BLK)]
        moved = jnp.dot(around, band_of(b), preferred_element_type=jnp.float32)
        for part in range(2):
            turned = moved[part * pulse_rows : (part + 1) * pulse_rows].T.astype(jnp.bfloat16)
            outgoing[pl.ds(b * peers, peers), part] = turned.reshape(peers, bins, pulse_rows)

    def send(b):
        def one(n, carry):
            peer = b * peers + n

            @pl.when(peer != me)
            def _():
                pltpu.make_async_remote_copy(
                    src_ref=outgoing.at[peer],
                    dst_ref=gathered.at[me + edge],
                    send_sem=send_sem,
                    recv_sem=recv_sem.at[me // group],
                    device_id=(peer, quarter),
                    device_id_type=MESH,
                ).start()

            return carry

        lax.fori_loop(0, peers, one, 0)

    half = blocks - range_steps + 1
    stride = blocks // 4
    compress(stride - 2, stride - 1)
    compress(stride, stride + 1)
    migrate(stride)
    migrate(stride - 1)

    neighbours = jnp.where(has_right, 1, 0) + jnp.where(has_left, 1, 0)
    pl.semaphore_wait(barrier, pulse_peers - 1 + neighbours)

    reach = right_halo.shape[2]
    to_left = pltpu.make_async_remote_copy(
        src_ref=own.at[:, :, pl.ds(0, reach)],
        dst_ref=right_halo,
        send_sem=halo_send_sem.at[0],
        recv_sem=halo_recv_sem.at[0],
        device_id=(me, quarter - 1),
        device_id_type=MESH,
    )
    to_right = pltpu.make_async_remote_copy(
        src_ref=own.at[:, :, pl.ds(quarter_len - BLK, BLK)],
        dst_ref=left_halo,
        send_sem=halo_send_sem.at[1],
        recv_sem=halo_recv_sem.at[1],
        device_id=(me, quarter + 1),
        device_id_type=MESH,
    )

    @pl.when(has_left)
    def _():
        to_left.start()

    @pl.when(has_right)
    def _():
        to_right.start()

    send(stride)
    send(stride - 1)
    compress(0, 1)

    def first(b, carry):
        migrate(b)
        send(b)
        return carry

    lax.fori_loop(1, stride - 1, first, 0)
    compress(half - 2, half - 1)
    place_toeplitz(azimuth_ref, azimuth_rows, azimuth_turned, azimuth_matrix)
    gathered[0:edge] = jnp.zeros((edge,) + gathered.shape[1:], jnp.bfloat16)
    gathered[edge + pulse_peers :] = jnp.zeros((edge,) + gathered.shape[1:], jnp.bfloat16)

    @pl.when(has_left)
    def _():
        to_right.wait_recv()
        join(left_halo, 0, 1)

    @pl.when(has_right)
    def _():
        to_left.wait_recv()
        join(right_halo, blocks + 1, reach // BLK)

    @pl.when(jnp.logical_not(has_left))
    def _():
        joined[0:pulse_rows, :] = jnp.zeros((pulse_rows, PAIR), jnp.bfloat16)

    @pl.when(jnp.logical_not(has_right))
    def _():
        rest = reach // BLK * pulse_rows
        joined[(blocks + 1) * pulse_rows :, :] = jnp.zeros((rest, PAIR), jnp.bfloat16)

    compress(-1, half)

    @pl.when(jnp.logical_not(has_left))
    def _():
        compressed[:, 0:BLK] = jnp.zeros((2 * pulse_rows, BLK), jnp.bfloat16)

    migrate(0)
    send(0)

    def second_pairs(i, carry):
        j = half + 1 + 2 * i
        compress(j, j + 1)
        return carry

    lax.fori_loop(0, (blocks - half) // 2, second_pairs, 0)

    def late(u, carry):
        b = half + u // 2 + stride * (u % 2)
        migrate(b)
        send(b)
        return carry

    lax.fori_loop(0, 2, late, 0)
    lax.fori_loop(stride + 1, half - 1, first, 0)
    lax.fori_loop(2, 6, late, 0)
    migrate(half - 1)
    send(half - 1)
    lax.fori_loop(6, 8, late, 0)

    keep = pltpu.make_async_copy(outgoing.at[me], gathered.at[me + edge], local_sem)
    keep.start()
    keep.wait()

    def arrive(g):
        for count, mine in ((group - 1, True), (group, False)):

            @pl.when((me // group == g) == mine)
            def _():
                pltpu.make_async_copy(
                    outgoing.at[pl.ds(0, count)], gathered.at[pl.ds(edge, count)], recv_sem.at[g]
                ).wait()

    def focus(start, count):
        window = jnp.concatenate(
            [
                gathered[pl.ds(start + k, count), part].reshape(count * bins, pulse_rows)
                for k in range(azimuth_steps)
                for part in range(2)
            ],
            axis=1,
        )
        result = jnp.dot(window, azimuth_matrix[...], preferred_element_type=jnp.float32)
        for n in range(count):
            at = pl.ds(pl.multiple_of((start + n) * BLK, BLK), BLK)
            for part in range(2):
                image[part, 0, :, at] = result[
                    n * bins : (n + 1) * bins, part * BLK : (part + 1) * BLK
                ]

    parity = me // group % 2
    even = parity == 0
    pairs = groups // 2

    def near(i, carry):
        g = 2 * i + parity
        arrive(g)
        focus(g * group + edge, group - 2 * edge)
        return carry

    def far(i, carry):
        g = 2 * i + 1 - parity
        arrive(g)
        over = jnp.where(even, jnp.where(i == pairs - 1, edge, 0), jnp.where(i == 0, -edge, 0))
        focus(g * group - edge - over, group + 2 * edge)
        return carry

    lax.fori_loop(0, pairs, near, 0)
    focus(jnp.where(even, 0, pulse_peers - 2 * edge), 2 * edge)
    lax.fori_loop(0, pairs, far, 0)

    @pl.when(has_left)
    def _():
        to_left.wait_send()

    @pl.when(has_right)
    def _():
        to_right.wait_send()

    others = pl.ds(0, pulse_peers - 1)
    pltpu.make_async_copy(outgoing.at[others], gathered.at[others], send_sem).wait()


def place_image(source, image, sem):
    copy = pltpu.make_async_copy(source, image, sem)
    copy.start()
    copy.wait()


def per_device(echoes, range_ref, band_weights, band_offsets, azimuth_ref):
    pulse_peers = lax.axis_size("pulse")
    quarters = lax.axis_size("rng")
    pulse_rows = echoes.shape[1]
    quarter_len = echoes.shape[2]
    blocks = quarter_len // BLK
    bins = quarter_len // pulse_peers
    range_blocks = range_ref.shape[1] // BLK
    azimuth_blocks = azimuth_ref.shape[1] // BLK
    reach = (range_blocks + 1) * BLK
    range_pad = -(-(2 * range_blocks + 2) // 8) * 8
    azimuth_pad = -(-(2 * azimuth_blocks + 2) // 8) * 8
    range_depth = (range_blocks + 1) * PAIR
    azimuth_depth = (azimuth_blocks + 1) * PAIR
    pulses = pulse_peers * pulse_rows
    groups = 8
    anywhere = pl.BlockSpec(memory_space=pl.ANY)
    in_vmem = pl.BlockSpec(memory_space=pltpu.VMEM)
    bf16 = jnp.bfloat16
    f32 = jnp.float32
    image_shape = (2, 1, bins, pulses)

    def kernel(*refs):
        focus_whole(pulse_peers, quarters, *refs)

    image = pl.pallas_call(
        kernel,
        out_shape=jax.ShapeDtypeStruct(image_shape, f32),
        in_specs=[anywhere] * 5,
        out_specs=in_vmem,
        scratch_shapes=[
            pltpu.VMEM((2, pulse_rows, quarter_len), bf16),
            pltpu.VMEM((2, pulse_rows, reach), bf16),
            pltpu.VMEM((2, pulse_rows, BLK), bf16),
            pltpu.VMEM(range_ref.shape, bf16),
            pltpu.VMEM(band_weights.shape, bf16),
            pltpu.VMEM((blocks, BLK), jnp.int32),
            pltpu.VMEM(azimuth_ref.shape, bf16),
            pltpu.VMEM(((blocks + 1 + reach // BLK) * pulse_rows, PAIR), bf16),
            pltpu.VMEM((range_pad, PAIR), f32),
            pltpu.VMEM((range_pad, PAIR), f32),
            pltpu.VMEM((range_depth, PAIR), bf16),
            pltpu.VMEM((azimuth_pad, PAIR), f32),
            pltpu.VMEM((azimuth_pad, PAIR), f32),
            pltpu.VMEM((azimuth_depth, PAIR), bf16),
            pltpu.VMEM((2 * pulse_rows, (blocks + 2) * BLK), bf16),
            pltpu.VMEM((pulse_peers, 2, bins, pulse_rows), bf16),
            pltpu.VMEM((pulse_peers + azimuth_blocks, 2, bins, pulse_rows), bf16),
            pltpu.SemaphoreType.DMA((5,)),
            pltpu.SemaphoreType.DMA((2,)),
            pltpu.SemaphoreType.DMA((2,)),
            pltpu.SemaphoreType.DMA,
            pltpu.SemaphoreType.DMA((groups,)),
            pltpu.SemaphoreType.DMA,
        ],
        compiler_params=pltpu.CompilerParams(
            collective_id=0, has_side_effects=True, vmem_limit_bytes=VMEM_BYTES
        ),
        name="focus_whole",
    )(
        *(
            pltpu.with_memory_space_constraint(operand, pltpu.HBM)
            for operand in (
                echoes,
                range_ref,
                band_weights,
                band_offsets.reshape(blocks, BLK),
                azimuth_ref,
            )
        )
    )

    return pl.pallas_call(
        place_image,
        out_shape=jax.ShapeDtypeStruct(image_shape, f32),
        in_specs=[in_vmem],
        out_specs=anywhere,
        scratch_shapes=[pltpu.SemaphoreType.DMA],
        compiler_params=pltpu.CompilerParams(vmem_limit_bytes=VMEM_BYTES),
        name="place_image",
    )(image)


def solution(mesh):
    return jax.shard_map(
        per_device,
        mesh=mesh,
        in_specs=(P(None, "pulse", "rng"), P(), P(None, "rng"), P("rng"), P()),
        out_specs=P(None, "rng", "pulse", None),
        check_vma=False,
    )
```

```python
import jax
import jax.numpy as jnp
from jax import lax
from jax.experimental import pallas as pl
from jax.experimental.pallas import tpu as pltpu
from jax.sharding import PartitionSpec as P

MESH = pl.DeviceIdType.MESH
BLK = 128
PAIR = 2 * BLK
VMEM_BYTES = 44 * 1024 * 1024


def place_toeplitz(taps_ref, rows_ref, turned_ref, matrix_ref):
    chunks = taps_ref.shape[1] // BLK
    rows_ref[...] = jnp.zeros_like(rows_ref)
    for k in range(chunks):
        chunk = taps_ref[:, k * BLK : (k + 1) * BLK].astype(jnp.float32)
        rows_ref[2 * k : 2 * k + 2, BLK:PAIR] = chunk
        rows_ref[2 * k + 2 : 2 * k + 4, 0:BLK] = chunk
    source = lax.broadcasted_iota(jnp.int32, (PAIR, PAIR), 0)
    lane = lax.broadcasted_iota(jnp.int32, (PAIR, PAIR), 1)
    wanted = jnp.where(lane < BLK, BLK - lane, 3 * BLK - lane)
    turn = jnp.where(source == wanted, 1.0, 0.0).astype(jnp.bfloat16)
    turned_ref[...] = jnp.dot(
        rows_ref[...].astype(jnp.bfloat16), turn, preferred_element_type=jnp.float32
    )
    for k in range(chunks + 1):
        tiles = []
        for part in range(2):
            row = turned_ref[2 * k + part : 2 * k + part + 1, :]
            spread = jnp.broadcast_to(row, (BLK, PAIR))
            tiles.append(pltpu.roll(spread, 0, 1, stride=1, stride_axis=0)[:, :BLK])
        real, imag = tiles
        top = k * PAIR
        matrix_ref[top : top + BLK, 0:BLK] = real.astype(jnp.bfloat16)
        matrix_ref[top : top + BLK, BLK:PAIR] = (-imag).astype(jnp.bfloat16)
        matrix_ref[top + BLK : top + PAIR, 0:BLK] = imag.astype(jnp.bfloat16)
        matrix_ref[top + BLK : top + PAIR, BLK:PAIR] = real.astype(jnp.bfloat16)


def focus_whole(
    pulse_peers,
    quarters,
    echoes_hbm,
    range_hbm,
    weights_hbm,
    offsets_hbm,
    azimuth_hbm,
    image,
    own,
    right_halo,
    left_halo,
    range_ref,
    weights,
    offsets,
    azimuth_ref,
    joined,
    range_rows,
    range_turned,
    range_matrix,
    azimuth_rows,
    azimuth_turned,
    azimuth_matrix,
    compressed,
    outgoing,
    gathered,
    load_sem,
    halo_send_sem,
    halo_recv_sem,
    send_sem,
    recv_sem,
    local_sem,
):
    me = lax.axis_index("pulse")
    quarter = lax.axis_index("rng")
    pulse_rows = own.shape[1]
    quarter_len = own.shape[2]
    blocks = quarter_len // BLK
    range_steps = range_matrix.shape[0] // PAIR
    azimuth_steps = azimuth_matrix.shape[0] // PAIR
    taps = weights.shape[0]
    bins = outgoing.shape[2]
    peers = BLK // bins
    groups = recv_sem.shape[0]
    group = pulse_peers // groups
    edge = (azimuth_steps - 1) // 2
    has_right = quarter < quarters - 1
    has_left = quarter > 0

    barrier = pltpu.get_barrier_semaphore()

    loads = [
        pltpu.make_async_copy(source, target, load_sem.at[n])
        for n, (source, target) in enumerate(
            (
                (range_hbm, range_ref),
                (echoes_hbm, own),
                (weights_hbm, weights),
                (offsets_hbm, offsets),
                (azimuth_hbm, azimuth_ref),
            )
        )
    ]
    for load in loads:
        load.start()

    @pl.when(has_right)
    def _():
        pl.semaphore_signal(barrier, inc=1, device_id=(me, quarter + 1), device_id_type=MESH)

    @pl.when(has_left)
    def _():
        pl.semaphore_signal(barrier, inc=1, device_id=(me, quarter - 1), device_id_type=MESH)

    def greet_one(step):
        peer = lax.rem(me + step, pulse_peers)
        pl.semaphore_signal(barrier, inc=1, device_id=(peer, quarter), device_id_type=MESH)

    run = 8

    def greet(turn, carry):
        for n in range(run):
            greet_one(turn * run + n + 1)
        return carry

    lax.fori_loop(0, (pulse_peers - 1) // run, greet, 0)
    for step in range((pulse_peers - 1) // run * run + 1, pulse_peers):
        greet_one(step)

    loads[0].wait()
    place_toeplitz(range_ref, range_rows, range_turned, range_matrix)
    for load in loads[1:]:
        load.wait()

    def join(source, first, count):
        for m in range(count):
            for part in range(2):
                joined[
                    (first + m) * pulse_rows : (first + m + 1) * pulse_rows,
                    part * BLK : (part + 1) * BLK,
                ] = source[part, :, m * BLK : (m + 1) * BLK]

    join(own, 1, blocks)

    def compress(*js):
        window = jnp.concatenate(
            [
                jnp.concatenate(
                    [
                        joined[
                            pl.ds(pl.multiple_of((j + 1 + k) * pulse_rows, pulse_rows), pulse_rows)
                        ]
                        for j in js
                    ],
                    axis=0,
                )
                for k in range(range_steps)
            ],
            axis=1,
        )
        block = jnp.dot(window, range_matrix[...], preferred_element_type=jnp.float32)
        block = block.astype(jnp.bfloat16)
        for n, j in enumerate(js):
            at = pl.ds(pl.multiple_of((j + 1) * BLK, BLK), BLK)
            for part in range(2):
                compressed[part * pulse_rows : (part + 1) * pulse_rows, at] = block[
                    n * pulse_rows : (n + 1) * pulse_rows, part * BLK : (part + 1) * BLK
                ]

    def band_of(b):
        start = BLK - BLK // 2 + taps // 2
        lane = lax.broadcasted_iota(jnp.int32, (8, BLK), 1)
        shift = jnp.broadcast_to(offsets[pl.ds(b, 1), :], (8, BLK)) + lane

        def shifted(bit, rows):
            return jnp.concatenate([(shift & bit) != 0] * (rows // 8), axis=0)

        table = weights[:, pl.ds(pl.multiple_of(b * BLK, BLK), BLK)].astype(jnp.float32)
        placed = jnp.concatenate([table, jnp.zeros((8, BLK), jnp.float32)], axis=0)
        for bit in (1, 2, 4):
            rows = placed.shape[0]
            placed = jnp.where(shifted(bit, rows), pltpu.roll(placed, bit, 0), placed)
        bit = 8
        while bit <= BLK - 1 + taps // 2:
            blank = jnp.zeros((bit, BLK), jnp.float32)
            lower = jnp.concatenate([blank, placed], axis=0)
            upper = jnp.concatenate([placed, blank], axis=0)
            placed = jnp.where(shifted(bit, lower.shape[0]), lower, upper)
            bit *= 2
        return jnp.concatenate(
            [jnp.zeros((start, BLK), jnp.float32), placed[: 3 * BLK - start]], axis=0
        ).astype(jnp.bfloat16)

    def migrate(b):
        around = compressed[:, pl.ds(pl.multiple_of(b * BLK, BLK), 3 * BLK)]
        moved = jnp.dot(around, band_of(b), preferred_element_type=jnp.float32)
        for part in range(2):
            turned = moved[part * pulse_rows : (part + 1) * pulse_rows].T.astype(jnp.bfloat16)
            outgoing[pl.ds(b * peers, peers), part] = turned.reshape(peers, bins, pulse_rows)

    def send(b):
        def one(n, carry):
            peer = b * peers + n

            @pl.when(peer != me)
            def _():
                pltpu.make_async_remote_copy(
                    src_ref=outgoing.at[peer],
                    dst_ref=gathered.at[me + edge],
                    send_sem=send_sem,
                    recv_sem=recv_sem.at[me // group],
                    device_id=(peer, quarter),
                    device_id_type=MESH,
                ).start()

            return carry

        lax.fori_loop(0, peers, one, 0)

    half = blocks - range_steps + 1
    stride = blocks // 4
    compress(stride - 2, stride - 1)
    compress(stride, stride + 1)
    migrate(stride)

    neighbours = jnp.where(has_right, 1, 0) + jnp.where(has_left, 1, 0)
    pl.semaphore_wait(barrier, pulse_peers - 1 + neighbours)

    reach = right_halo.shape[2]
    to_left = pltpu.make_async_remote_copy(
        src_ref=own.at[:, :, pl.ds(0, reach)],
        dst_ref=right_halo,
        send_sem=halo_send_sem.at[0],
        recv_sem=halo_recv_sem.at[0],
        device_id=(me, quarter - 1),
        device_id_type=MESH,
    )
    to_right = pltpu.make_async_remote_copy(
        src_ref=own.at[:, :, pl.ds(quarter_len - BLK, BLK)],
        dst_ref=left_halo,
        send_sem=halo_send_sem.at[1],
        recv_sem=halo_recv_sem.at[1],
        device_id=(me, quarter + 1),
        device_id_type=MESH,
    )

    @pl.when(has_left)
    def _():
        to_left.start()

    @pl.when(has_right)
    def _():
        to_right.start()

    send(stride)
    migrate(stride - 1)
    send(stride - 1)
    compress(0, 1)

    def first(b, carry):
        migrate(b)
        send(b)
        return carry

    lax.fori_loop(1, stride - 1, first, 0)
    compress(half - 2, half - 1)
    place_toeplitz(azimuth_ref, azimuth_rows, azimuth_turned, azimuth_matrix)
    gathered[0:edge] = jnp.zeros((edge,) + gathered.shape[1:], jnp.bfloat16)
    gathered[edge + pulse_peers :] = jnp.zeros((edge,) + gathered.shape[1:], jnp.bfloat16)

    @pl.when(has_left)
    def _():
        to_right.wait_recv()
        join(left_halo, 0, 1)

    @pl.when(has_right)
    def _():
        to_left.wait_recv()
        join(right_halo, blocks + 1, reach // BLK)

    @pl.when(jnp.logical_not(has_left))
    def _():
        joined[0:pulse_rows, :] = jnp.zeros((pulse_rows, PAIR), jnp.bfloat16)

    @pl.when(jnp.logical_not(has_right))
    def _():
        rest = reach // BLK * pulse_rows
        joined[(blocks + 1) * pulse_rows :, :] = jnp.zeros((rest, PAIR), jnp.bfloat16)

    compress(-1, half)

    @pl.when(jnp.logical_not(has_left))
    def _():
        compressed[:, 0:BLK] = jnp.zeros((2 * pulse_rows, BLK), jnp.bfloat16)

    migrate(0)
    send(0)

    def second_pairs(i, carry):
        j = half + 1 + 2 * i
        compress(j, j + 1)
        return carry

    lax.fori_loop(0, (blocks - half) // 2, second_pairs, 0)

    def late(u, carry):
        b = half + u // 2 + stride * (u % 2)
        migrate(b)
        send(b)
        return carry

    lax.fori_loop(0, 2, late, 0)
    lax.fori_loop(stride + 1, half - 1, first, 0)
    lax.fori_loop(2, 6, late, 0)
    migrate(half - 1)
    send(half - 1)
    lax.fori_loop(6, 8, late, 0)

    keep = pltpu.make_async_copy(outgoing.at[me], gathered.at[me + edge], local_sem)
    keep.start()
    keep.wait()

    def arrive(g):
        for count, mine in ((group - 1, True), (group, False)):

            @pl.when((me // group == g) == mine)
            def _():
                pltpu.make_async_copy(
                    outgoing.at[pl.ds(0, count)], gathered.at[pl.ds(edge, count)], recv_sem.at[g]
                ).wait()

    def focus(start, count):
        window = jnp.concatenate(
            [
                gathered[pl.ds(start + k, count), part].reshape(count * bins, pulse_rows)
                for k in range(azimuth_steps)
                for part in range(2)
            ],
            axis=1,
        )
        result = jnp.dot(window, azimuth_matrix[...], preferred_element_type=jnp.float32)
        for n in range(count):
            at = pl.ds(pl.multiple_of((start + n) * BLK, BLK), BLK)
            for part in range(2):
                image[part, 0, :, at] = result[
                    n * bins : (n + 1) * bins, part * BLK : (part + 1) * BLK
                ]

    parity = me // group % 2
    even = parity == 0
    pairs = groups // 2

    def near(i, carry):
        g = 2 * i + parity
        arrive(g)
        focus(g * group + edge, group - 2 * edge)
        return carry

    def far(i, carry):
        g = 2 * i + 1 - parity
        arrive(g)
        over = jnp.where(even, jnp.where(i == pairs - 1, edge, 0), jnp.where(i == 0, -edge, 0))
        focus(g * group - edge - over, group + 2 * edge)
        return carry

    lax.fori_loop(0, pairs, near, 0)
    focus(jnp.where(even, 0, pulse_peers - 2 * edge), 2 * edge)
    lax.fori_loop(0, pairs, far, 0)

    @pl.when(has_left)
    def _():
        to_left.wait_send()

    @pl.when(has_right)
    def _():
        to_right.wait_send()

    others = pl.ds(0, pulse_peers - 1)
    pltpu.make_async_copy(outgoing.at[others], gathered.at[others], send_sem).wait()


def place_image(source, image, sem):
    copy = pltpu.make_async_copy(source, image, sem)
    copy.start()
    copy.wait()


def per_device(echoes, range_ref, band_weights, band_offsets, azimuth_ref):
    pulse_peers = lax.axis_size("pulse")
    quarters = lax.axis_size("rng")
    pulse_rows = echoes.shape[1]
    quarter_len = echoes.shape[2]
    blocks = quarter_len // BLK
    bins = quarter_len // pulse_peers
    range_blocks = range_ref.shape[1] // BLK
    azimuth_blocks = azimuth_ref.shape[1] // BLK
    reach = (range_blocks + 1) * BLK
    range_pad = -(-(2 * range_blocks + 2) // 8) * 8
    azimuth_pad = -(-(2 * azimuth_blocks + 2) // 8) * 8
    range_depth = (range_blocks + 1) * PAIR
    azimuth_depth = (azimuth_blocks + 1) * PAIR
    pulses = pulse_peers * pulse_rows
    groups = 8
    anywhere = pl.BlockSpec(memory_space=pl.ANY)
    in_vmem = pl.BlockSpec(memory_space=pltpu.VMEM)
    bf16 = jnp.bfloat16
    f32 = jnp.float32
    image_shape = (2, 1, bins, pulses)

    def kernel(*refs):
        focus_whole(pulse_peers, quarters, *refs)

    image = pl.pallas_call(
        kernel,
        out_shape=jax.ShapeDtypeStruct(image_shape, f32),
        in_specs=[anywhere] * 5,
        out_specs=in_vmem,
        scratch_shapes=[
            pltpu.VMEM((2, pulse_rows, quarter_len), bf16),
            pltpu.VMEM((2, pulse_rows, reach), bf16),
            pltpu.VMEM((2, pulse_rows, BLK), bf16),
            pltpu.VMEM(range_ref.shape, bf16),
            pltpu.VMEM(band_weights.shape, bf16),
            pltpu.VMEM((blocks, BLK), jnp.int32),
            pltpu.VMEM(azimuth_ref.shape, bf16),
            pltpu.VMEM(((blocks + 1 + reach // BLK) * pulse_rows, PAIR), bf16),
            pltpu.VMEM((range_pad, PAIR), f32),
            pltpu.VMEM((range_pad, PAIR), f32),
            pltpu.VMEM((range_depth, PAIR), bf16),
            pltpu.VMEM((azimuth_pad, PAIR), f32),
            pltpu.VMEM((azimuth_pad, PAIR), f32),
            pltpu.VMEM((azimuth_depth, PAIR), bf16),
            pltpu.VMEM((2 * pulse_rows, (blocks + 2) * BLK), bf16),
            pltpu.VMEM((pulse_peers, 2, bins, pulse_rows), bf16),
            pltpu.VMEM((pulse_peers + azimuth_blocks, 2, bins, pulse_rows), bf16),
            pltpu.SemaphoreType.DMA((5,)),
            pltpu.SemaphoreType.DMA((2,)),
            pltpu.SemaphoreType.DMA((2,)),
            pltpu.SemaphoreType.DMA,
            pltpu.SemaphoreType.DMA((groups,)),
            pltpu.SemaphoreType.DMA,
        ],
        compiler_params=pltpu.CompilerParams(
            collective_id=0, has_side_effects=True, vmem_limit_bytes=VMEM_BYTES
        ),
        name="focus_whole",
    )(
        *(
            pltpu.with_memory_space_constraint(operand, pltpu.HBM)
            for operand in (
                echoes,
                range_ref,
                band_weights,
                band_offsets.reshape(blocks, BLK),
                azimuth_ref,
            )
        )
    )

    return pl.pallas_call(
        place_image,
        out_shape=jax.ShapeDtypeStruct(image_shape, f32),
        in_specs=[in_vmem],
        out_specs=anywhere,
        scratch_shapes=[pltpu.SemaphoreType.DMA],
        compiler_params=pltpu.CompilerParams(vmem_limit_bytes=VMEM_BYTES),
        name="place_image",
    )(image)


def solution(mesh):
    return jax.shard_map(
        per_device,
        mesh=mesh,
        in_specs=(P(None, "pulse", "rng"), P(), P(None, "rng"), P("rng"), P()),
        out_specs=P(None, "rng", "pulse", None),
        check_vma=False,
    )
```

```python
import jax
import jax.numpy as jnp
from jax import lax
from jax.experimental import pallas as pl
from jax.experimental.pallas import tpu as pltpu
from jax.sharding import PartitionSpec as P

MESH = pl.DeviceIdType.MESH
BLK = 128
PAIR = 2 * BLK
VMEM_BYTES = 44 * 1024 * 1024


def place_toeplitz(taps_ref, rows_ref, turned_ref, matrix_ref):
    chunks = taps_ref.shape[1] // BLK
    rows_ref[...] = jnp.zeros_like(rows_ref)
    for k in range(chunks):
        chunk = taps_ref[:, k * BLK : (k + 1) * BLK].astype(jnp.float32)
        rows_ref[2 * k : 2 * k + 2, BLK:PAIR] = chunk
        rows_ref[2 * k + 2 : 2 * k + 4, 0:BLK] = chunk
    source = lax.broadcasted_iota(jnp.int32, (PAIR, PAIR), 0)
    lane = lax.broadcasted_iota(jnp.int32, (PAIR, PAIR), 1)
    wanted = jnp.where(lane < BLK, BLK - lane, 3 * BLK - lane)
    turn = jnp.where(source == wanted, 1.0, 0.0).astype(jnp.bfloat16)
    turned_ref[...] = jnp.dot(
        rows_ref[...].astype(jnp.bfloat16), turn, preferred_element_type=jnp.float32
    )
    for k in range(chunks + 1):
        tiles = []
        for part in range(2):
            row = turned_ref[2 * k + part : 2 * k + part + 1, :]
            spread = jnp.broadcast_to(row, (BLK, PAIR))
            tiles.append(pltpu.roll(spread, 0, 1, stride=1, stride_axis=0)[:, :BLK])
        real, imag = tiles
        top = k * PAIR
        matrix_ref[top : top + BLK, 0:BLK] = real.astype(jnp.bfloat16)
        matrix_ref[top : top + BLK, BLK:PAIR] = (-imag).astype(jnp.bfloat16)
        matrix_ref[top + BLK : top + PAIR, 0:BLK] = imag.astype(jnp.bfloat16)
        matrix_ref[top + BLK : top + PAIR, BLK:PAIR] = real.astype(jnp.bfloat16)


def focus_whole(
    pulse_peers,
    quarters,
    echoes_hbm,
    range_hbm,
    weights_hbm,
    offsets_hbm,
    azimuth_hbm,
    image,
    own,
    right_halo,
    left_halo,
    range_ref,
    weights,
    offsets,
    azimuth_ref,
    joined,
    range_rows,
    range_turned,
    range_matrix,
    azimuth_rows,
    azimuth_turned,
    azimuth_matrix,
    compressed,
    outgoing,
    gathered,
    load_sem,
    halo_send_sem,
    halo_recv_sem,
    send_sem,
    recv_sem,
    local_sem,
):
    me = lax.axis_index("pulse")
    quarter = lax.axis_index("rng")
    pulse_rows = own.shape[1]
    quarter_len = own.shape[2]
    blocks = quarter_len // BLK
    range_steps = range_matrix.shape[0] // PAIR
    azimuth_steps = azimuth_matrix.shape[0] // PAIR
    taps = weights.shape[0]
    bins = outgoing.shape[2]
    peers = BLK // bins
    groups = recv_sem.shape[0]
    group = pulse_peers // groups
    edge = (azimuth_steps - 1) // 2
    has_right = quarter < quarters - 1
    has_left = quarter > 0

    barrier = pltpu.get_barrier_semaphore()

    loads = [
        pltpu.make_async_copy(source, target, load_sem.at[n])
        for n, (source, target) in enumerate(
            (
                (range_hbm, range_ref),
                (echoes_hbm, own),
                (weights_hbm, weights),
                (offsets_hbm, offsets),
                (azimuth_hbm, azimuth_ref),
            )
        )
    ]
    for load in loads:
        load.start()

    @pl.when(has_right)
    def _():
        pl.semaphore_signal(barrier, inc=1, device_id=(me, quarter + 1), device_id_type=MESH)

    @pl.when(has_left)
    def _():
        pl.semaphore_signal(barrier, inc=1, device_id=(me, quarter - 1), device_id_type=MESH)

    def greet_one(step):
        peer = lax.rem(me + step, pulse_peers)
        pl.semaphore_signal(barrier, inc=1, device_id=(peer, quarter), device_id_type=MESH)

    run = 8

    def greet(turn, carry):
        for n in range(run):
            greet_one(turn * run + n + 1)
        return carry

    lax.fori_loop(0, (pulse_peers - 1) // run, greet, 0)
    for step in range((pulse_peers - 1) // run * run + 1, pulse_peers):
        greet_one(step)

    loads[0].wait()
    place_toeplitz(range_ref, range_rows, range_turned, range_matrix)
    for load in loads[1:]:
        load.wait()

    def join(source, first, count):
        for m in range(count):
            for part in range(2):
                joined[
                    (first + m) * pulse_rows : (first + m + 1) * pulse_rows,
                    part * BLK : (part + 1) * BLK,
                ] = source[part, :, m * BLK : (m + 1) * BLK]

    join(own, 1, blocks)

    def compress(*js):
        window = jnp.concatenate(
            [
                jnp.concatenate(
                    [
                        joined[
                            pl.ds(pl.multiple_of((j + 1 + k) * pulse_rows, pulse_rows), pulse_rows)
                        ]
                        for j in js
                    ],
                    axis=0,
                )
                for k in range(range_steps)
            ],
            axis=1,
        )
        block = jnp.dot(window, range_matrix[...], preferred_element_type=jnp.float32)
        block = block.astype(jnp.bfloat16)
        for n, j in enumerate(js):
            at = pl.ds(pl.multiple_of((j + 1) * BLK, BLK), BLK)
            for part in range(2):
                compressed[part * pulse_rows : (part + 1) * pulse_rows, at] = block[
                    n * pulse_rows : (n + 1) * pulse_rows, part * BLK : (part + 1) * BLK
                ]

    def band_of(b):
        start = BLK - BLK // 2 + taps // 2
        lane = lax.broadcasted_iota(jnp.int32, (8, BLK), 1)
        shift = jnp.broadcast_to(offsets[pl.ds(b, 1), :], (8, BLK)) + lane

        def shifted(bit, rows):
            return jnp.concatenate([(shift & bit) != 0] * (rows // 8), axis=0)

        table = weights[:, pl.ds(pl.multiple_of(b * BLK, BLK), BLK)].astype(jnp.float32)
        placed = jnp.concatenate([table, jnp.zeros((8, BLK), jnp.float32)], axis=0)
        for bit in (1, 2, 4):
            rows = placed.shape[0]
            placed = jnp.where(shifted(bit, rows), pltpu.roll(placed, bit, 0), placed)
        bit = 8
        while bit <= BLK - 1 + taps // 2:
            blank = jnp.zeros((bit, BLK), jnp.float32)
            lower = jnp.concatenate([blank, placed], axis=0)
            upper = jnp.concatenate([placed, blank], axis=0)
            placed = jnp.where(shifted(bit, lower.shape[0]), lower, upper)
            bit *= 2
        return jnp.concatenate(
            [jnp.zeros((start, BLK), jnp.float32), placed[: 3 * BLK - start]], axis=0
        ).astype(jnp.bfloat16)

    def migrate(b):
        around = compressed[:, pl.ds(pl.multiple_of(b * BLK, BLK), 3 * BLK)]
        moved = jnp.dot(around, band_of(b), preferred_element_type=jnp.float32)
        for part in range(2):
            turned = moved[part * pulse_rows : (part + 1) * pulse_rows].T.astype(jnp.bfloat16)
            outgoing[pl.ds(b * peers, peers), part] = turned.reshape(peers, bins, pulse_rows)

    def send(b):
        def one(n, carry):
            peer = b * peers + n

            @pl.when(peer != me)
            def _():
                pltpu.make_async_remote_copy(
                    src_ref=outgoing.at[peer],
                    dst_ref=gathered.at[me + edge],
                    send_sem=send_sem,
                    recv_sem=recv_sem.at[me // group],
                    device_id=(peer, quarter),
                    device_id_type=MESH,
                ).start()

            return carry

        lax.fori_loop(0, peers, one, 0)

    half = blocks - range_steps + 1
    stride = blocks // 4
    compress(stride - 2, stride - 1)
    compress(stride, stride + 1)
    migrate(stride)

    neighbours = jnp.where(has_right, 1, 0) + jnp.where(has_left, 1, 0)
    pl.semaphore_wait(barrier, pulse_peers - 1 + neighbours)

    reach = right_halo.shape[2]
    to_left = pltpu.make_async_remote_copy(
        src_ref=own.at[:, :, pl.ds(0, reach)],
        dst_ref=right_halo,
        send_sem=halo_send_sem.at[0],
        recv_sem=halo_recv_sem.at[0],
        device_id=(me, lax.rem(quarter + quarters - 1, quarters)),
        device_id_type=MESH,
    )
    to_right = pltpu.make_async_remote_copy(
        src_ref=own.at[:, :, pl.ds(quarter_len - BLK, BLK)],
        dst_ref=left_halo,
        send_sem=halo_send_sem.at[1],
        recv_sem=halo_recv_sem.at[1],
        device_id=(me, lax.rem(quarter + 1, quarters)),
        device_id_type=MESH,
    )

    @pl.when(has_left)
    def _():
        to_left.start()

    @pl.when(has_right)
    def _():
        to_right.start()

    send(stride)
    migrate(stride - 1)
    send(stride - 1)
    compress(0, 1)

    def first(b, carry):
        migrate(b)
        send(b)
        return carry

    lax.fori_loop(1, stride - 1, first, 0)
    compress(half - 2, half - 1)
    place_toeplitz(azimuth_ref, azimuth_rows, azimuth_turned, azimuth_matrix)
    gathered[0:edge] = jnp.zeros((edge,) + gathered.shape[1:], jnp.bfloat16)
    gathered[edge + pulse_peers :] = jnp.zeros((edge,) + gathered.shape[1:], jnp.bfloat16)

    @pl.when(has_left)
    def _():
        to_right.wait_recv()
        join(left_halo, 0, 1)

    @pl.when(has_right)
    def _():
        to_left.wait_recv()
        join(right_halo, blocks + 1, reach // BLK)

    @pl.when(jnp.logical_not(has_left))
    def _():
        joined[0:pulse_rows, :] = jnp.zeros((pulse_rows, PAIR), jnp.bfloat16)

    @pl.when(jnp.logical_not(has_right))
    def _():
        rest = reach // BLK * pulse_rows
        joined[(blocks + 1) * pulse_rows :, :] = jnp.zeros((rest, PAIR), jnp.bfloat16)

    compress(-1, half)

    @pl.when(jnp.logical_not(has_left))
    def _():
        compressed[:, 0:BLK] = jnp.zeros((2 * pulse_rows, BLK), jnp.bfloat16)

    migrate(0)
    send(0)

    def second_pairs(i, carry):
        j = half + 1 + 2 * i
        compress(j, j + 1)
        return carry

    lax.fori_loop(0, (blocks - half) // 2, second_pairs, 0)

    def late(u, carry):
        b = half + u // 2 + stride * (u % 2)
        migrate(b)
        send(b)
        return carry

    lax.fori_loop(0, 2, late, 0)
    lax.fori_loop(stride + 1, half - 1, first, 0)
    lax.fori_loop(2, 6, late, 0)
    migrate(half - 1)
    send(half - 1)
    lax.fori_loop(6, 8, late, 0)

    keep = pltpu.make_async_copy(outgoing.at[me], gathered.at[me + edge], local_sem)
    keep.start()
    keep.wait()

    def arrive(g):
        for count, mine in ((group - 1, True), (group, False)):

            @pl.when((me // group == g) == mine)
            def _():
                pltpu.make_async_copy(
                    outgoing.at[pl.ds(0, count)], gathered.at[pl.ds(edge, count)], recv_sem.at[g]
                ).wait()

    def focus(start, count):
        window = jnp.concatenate(
            [
                gathered[pl.ds(start + k, count), part].reshape(count * bins, pulse_rows)
                for k in range(azimuth_steps)
                for part in range(2)
            ],
            axis=1,
        )
        result = jnp.dot(window, azimuth_matrix[...], preferred_element_type=jnp.float32)
        for n in range(count):
            at = pl.ds(pl.multiple_of((start + n) * BLK, BLK), BLK)
            for part in range(2):
                image[part, 0, :, at] = result[
                    n * bins : (n + 1) * bins, part * BLK : (part + 1) * BLK
                ]

    parity = me // group % 2
    even = parity == 0
    pairs = groups // 2

    def near(i, carry):
        g = 2 * i + parity
        arrive(g)
        focus(g * group + edge, group - 2 * edge)
        return carry

    def far(i, carry):
        g = 2 * i + 1 - parity
        arrive(g)
        over = jnp.where(even, jnp.where(i == pairs - 1, edge, 0), jnp.where(i == 0, -edge, 0))
        focus(g * group - edge - over, group + 2 * edge)
        return carry

    lax.fori_loop(0, pairs, near, 0)
    focus(jnp.where(even, 0, pulse_peers - 2 * edge), 2 * edge)
    lax.fori_loop(0, pairs, far, 0)

    @pl.when(has_left)
    def _():
        to_left.wait_send()

    @pl.when(has_right)
    def _():
        to_right.wait_send()

    others = pl.ds(0, pulse_peers - 1)
    pltpu.make_async_copy(outgoing.at[others], gathered.at[others], send_sem).wait()


def place_image(source, image, sem):
    copy = pltpu.make_async_copy(source, image, sem)
    copy.start()
    copy.wait()


def per_device(echoes, range_ref, band_weights, band_offsets, azimuth_ref):
    pulse_peers = lax.axis_size("pulse")
    quarters = lax.axis_size("rng")
    pulse_rows = echoes.shape[1]
    quarter_len = echoes.shape[2]
    blocks = quarter_len // BLK
    bins = quarter_len // pulse_peers
    range_blocks = range_ref.shape[1] // BLK
    azimuth_blocks = azimuth_ref.shape[1] // BLK
    reach = (range_blocks + 1) * BLK
    range_pad = -(-(2 * range_blocks + 2) // 8) * 8
    azimuth_pad = -(-(2 * azimuth_blocks + 2) // 8) * 8
    range_depth = (range_blocks + 1) * PAIR
    azimuth_depth = (azimuth_blocks + 1) * PAIR
    pulses = pulse_peers * pulse_rows
    groups = 8
    anywhere = pl.BlockSpec(memory_space=pl.ANY)
    in_vmem = pl.BlockSpec(memory_space=pltpu.VMEM)
    bf16 = jnp.bfloat16
    f32 = jnp.float32
    image_shape = (2, 1, bins, pulses)

    def kernel(*refs):
        focus_whole(pulse_peers, quarters, *refs)

    image = pl.pallas_call(
        kernel,
        out_shape=jax.ShapeDtypeStruct(image_shape, f32),
        in_specs=[anywhere] * 5,
        out_specs=in_vmem,
        scratch_shapes=[
            pltpu.VMEM((2, pulse_rows, quarter_len), bf16),
            pltpu.VMEM((2, pulse_rows, reach), bf16),
            pltpu.VMEM((2, pulse_rows, BLK), bf16),
            pltpu.VMEM(range_ref.shape, bf16),
            pltpu.VMEM(band_weights.shape, bf16),
            pltpu.VMEM((blocks, BLK), jnp.int32),
            pltpu.VMEM(azimuth_ref.shape, bf16),
            pltpu.VMEM(((blocks + 1 + reach // BLK) * pulse_rows, PAIR), bf16),
            pltpu.VMEM((range_pad, PAIR), f32),
            pltpu.VMEM((range_pad, PAIR), f32),
            pltpu.VMEM((range_depth, PAIR), bf16),
            pltpu.VMEM((azimuth_pad, PAIR), f32),
            pltpu.VMEM((azimuth_pad, PAIR), f32),
            pltpu.VMEM((azimuth_depth, PAIR), bf16),
            pltpu.VMEM((2 * pulse_rows, (blocks + 2) * BLK), bf16),
            pltpu.VMEM((pulse_peers, 2, bins, pulse_rows), bf16),
            pltpu.VMEM((pulse_peers + azimuth_blocks, 2, bins, pulse_rows), bf16),
            pltpu.SemaphoreType.DMA((5,)),
            pltpu.SemaphoreType.DMA((2,)),
            pltpu.SemaphoreType.DMA((2,)),
            pltpu.SemaphoreType.DMA,
            pltpu.SemaphoreType.DMA((groups,)),
            pltpu.SemaphoreType.DMA,
        ],
        compiler_params=pltpu.CompilerParams(
            collective_id=0, has_side_effects=True, vmem_limit_bytes=VMEM_BYTES
        ),
        name="focus_whole",
    )(
        *(
            pltpu.with_memory_space_constraint(operand, pltpu.HBM)
            for operand in (
                echoes,
                range_ref,
                band_weights,
                band_offsets.reshape(blocks, BLK),
                azimuth_ref,
            )
        )
    )

    return pl.pallas_call(
        place_image,
        out_shape=jax.ShapeDtypeStruct(image_shape, f32),
        in_specs=[in_vmem],
        out_specs=anywhere,
        scratch_shapes=[pltpu.SemaphoreType.DMA],
        compiler_params=pltpu.CompilerParams(vmem_limit_bytes=VMEM_BYTES),
        name="place_image",
    )(image)


def solution(mesh):
    return jax.shard_map(
        per_device,
        mesh=mesh,
        in_specs=(P(None, "pulse", "rng"), P(), P(None, "rng"), P("rng"), P()),
        out_specs=P(None, "rng", "pulse", None),
        check_vma=False,
    )
```
